32 devices in a mesh: slab: 2 (over y), patch: 4 (over z), atom: 2 (over core), feat: 2 (over x).
Axes of the slice: x: 2, y: 2, z: 4, core: 2. Of those that a mesh axis runs over, the one named last changes fastest.
Arguments:
- patches: bfloat16 [3072, 1728], P(('slab', 'patch'), 'feat'), parts along dimension 0, may hold values from -160 to 160
- dictionary: bfloat16 [1728, 2048], P('feat', 'atom'), may hold values from -0.15625 to 0.15625
- threshold: float32 [2048], P('atom'), may hold values from 0.05 to 0.5
Outputs:
- codes: bfloat16 [3072, 2048], P(('slab', 'patch'), 'atom'), parts along dimension 0
- gram: float32 [4096, 2048], P(('slab', 'atom', 'feat'), 'patch'), parts along dimension 0
- cross: float32 [3456, 2048], P(('slab', 'feat'), ('patch', 'atom')), parts along dimension 0
The draws below stay inside these ranges and needn't reach their ends.
There are 2 independent parts, one for each index of `slab`. The reference program is written for one: setup_inputs(seed, part) draws one part's arguments, and reference() takes and returns one part's arrays. A program takes and returns all parts, laid end to end along the dimension named above; an argument that names none is the same for every part. Nothing has to cross between parts.
All inputs are finite; a program needn't handle non-finite values.
Results may differ from the reference program's by a relative error of at most 0.011.
Values may be sent and summed in bfloat16 or wider, within the bound.
No kernel may reach another device: no remote copies, remote signals or barrier semaphores. Data moves between devices by JAX's collectives and lax.ppermute only.
A program may use at most 64 MiB of HBM per device.

```python
import math
import jax
import jax.numpy as jnp
from jax import lax

BINS = 8
VOXELS = 216
ATOMS = 2048
LENGTH = 1728
PATCHES = 1536


def draw_patches(key, part):
    key = jax.random.fold_in(key, 11)
    row_key, base_key = jax.random.split(key, 2)
    rows = jnp.exp(jax.random.uniform(row_key, (PATCHES, 1), jnp.float32) * jnp.log(10.0))
    levels = 3.0 ** (jnp.arange(BINS, dtype=jnp.float32) / max(BINS - 1, 1))
    columns = jnp.repeat(levels, VOXELS)[None, :]
    base = jnp.clip(jax.random.normal(base_key, (PATCHES, LENGTH), jnp.float32), -5.0, 5.0)
    return (base * rows * columns).astype(jnp.bfloat16)


def steps_of(rng, shape, pieces, smallest, largest):
    factor_of, own = 1.0, jax.random.fold_in(rng, 6)
    for dim, blocks in pieces:
        draws = jnp.exp(jax.random.uniform(jax.random.fold_in(own, dim), (blocks,), jnp.float32, smallest / len(pieces), largest / len(pieces)))
        factor_of = factor_of * jnp.repeat(draws, shape[dim] // blocks).reshape([-1 if axis == dim else 1 for axis in range(len(shape))])
    return factor_of


def gaussian(stream_key, shape, width, most, cuts=(), held_as=jnp.bfloat16):
    loudness = steps_of(stream_key, shape, cuts, -0.22, 0.18) if cuts else 1.0
    values = jax.random.normal(stream_key, shape, jnp.float32) * width * loudness
    return jnp.minimum(jnp.maximum(values, -most), most).astype(held_as)


def setup_inputs(seed: int = 0, part: int = 0) -> dict:
    splits = jax.random.split(jax.random.key(seed), 4)
    part_splits = jax.random.split(jax.random.fold_in(splits[3], part), 4)
    patches = draw_patches(jax.random.fold_in(jax.random.fold_in(splits[3], part), 71), part)
    dictionary = gaussian(splits[1], (LENGTH, ATOMS), LENGTH ** -0.5, 0.15625, ((0, 2), (1, 2)))
    threshold = jnp.clip(jnp.exp(math.log(0.5) - 2.3025851 * jax.random.uniform(splits[2], (ATOMS,), jnp.float32) ** steps_of(splits[2], (ATOMS,), ((0, 2),), -0.2, 0.2)), 0.05, 0.5)
    return dict(patches=patches, dictionary=dictionary, threshold=threshold)


step_rate = 0.2

def soften(value, level):
    return jnp.sign(value) * jnp.maximum(jnp.abs(value) - level, 0.0)

def reference(patches, dictionary, threshold):
    values = patches.astype(jnp.float32)
    scale = lax.rsqrt(lax.optimization_barrier(jnp.mean(values * values, axis=1, keepdims=True)) + 1e-05)
    first = scale * jnp.dot(patches, dictionary, preferred_element_type=jnp.float32)
    start = soften(step_rate * first, step_rate * threshold[None, :]).astype(jnp.bfloat16)
    rebuilt = lax.dot_general(start, dictionary, (((1,), (1,)), ((), ())), preferred_element_type=jnp.float32)
    misfit = (scale * values - rebuilt).astype(jnp.bfloat16)
    second = jnp.dot(misfit, dictionary, preferred_element_type=jnp.float32)
    codes = soften(start.astype(jnp.float32) + step_rate * second, step_rate * threshold[None, :]).astype(jnp.bfloat16)
    normed = (scale * values).astype(jnp.bfloat16)
    gram = lax.dot_general(codes, codes, (((0,), (0,)), ((), ())), preferred_element_type=jnp.float32) / PATCHES
    cross = lax.dot_general(normed, codes, (((0,), (0,)), ((), ())), preferred_element_type=jnp.float32) / PATCHES
    return (codes, gram, cross)
```

```python
import jax
import jax.numpy as jnp
from jax import lax
from jax.sharding import PartitionSpec as P

BINS = 8
VOXELS = 216


step_rate = 0.2
CHUNKS = 2


def soften(value, level):
    return jnp.sign(value) * jnp.maximum(jnp.abs(value) - level, 0.0)


def general(patches, dictionary, threshold):
    values = patches.astype(jnp.float32)
    local_sq = jnp.sum(values * values, axis=1)
    local_first = jnp.dot(patches, dictionary, preferred_element_type=jnp.float32)
    summed, energy = lax.psum((local_first, local_sq), "feat")
    scale = lax.rsqrt(energy[:, None] / (BINS * VOXELS) + 1e-05)
    level = step_rate * threshold[None, :]
    start = soften(step_rate * (scale * summed), level).astype(jnp.bfloat16)
    contract_last = (((1,), (1,)), ((), ()))
    own_part = lax.dot_general(start, dictionary, contract_last, preferred_element_type=jnp.float32)
    rebuilt = lax.psum(own_part, "atom")
    misfit = (scale * values - rebuilt).astype(jnp.bfloat16)
    local_second = jnp.dot(misfit, dictionary, preferred_element_type=jnp.float32)
    second = lax.psum(local_second, "feat")
    codes = soften(start.astype(jnp.float32) + step_rate * second, level).astype(jnp.bfloat16)
    codes_whole = lax.all_gather(codes, "atom", axis=1, tiled=True)
    n_patch = lax.axis_size("patch")
    n_atom = lax.axis_size("atom")
    n_feat = lax.axis_size("feat")
    total_atoms = codes_whole.shape[1]
    count = patches.shape[0] * n_patch
    contract_first = (((0,), (0,)), ((), ()))
    block_rows = total_atoms // (n_atom * n_feat)
    offset = (lax.axis_index("atom") * n_feat + lax.axis_index("feat")) * block_rows
    chosen = lax.dynamic_slice_in_dim(codes_whole, offset, block_rows, 1)
    gram_part = lax.dot_general(
        chosen, codes_whole, contract_first, preferred_element_type=jnp.float32
    )
    gram = (
        lax.psum_scatter(
            gram_part.astype(jnp.bfloat16), "patch", scatter_dimension=1, tiled=True
        ).astype(jnp.float32)
        / count
    )
    width = total_atoms // (n_patch * n_atom)
    arranged = codes_whole.reshape(codes_whole.shape[0], n_patch, n_atom, width)
    picked = lax.dynamic_slice_in_dim(arranged, lax.axis_index("atom"), 1, 2).reshape(
        codes_whole.shape[0], n_patch * width
    )
    normed = (scale * values).astype(jnp.bfloat16)
    cross_part = lax.dot_general(normed, picked, contract_first, preferred_element_type=jnp.float32)
    cross = (
        lax.psum_scatter(
            cross_part.astype(jnp.bfloat16), "patch", scatter_dimension=1, tiled=True
        ).astype(jnp.float32)
        / count
    )
    return (codes, gram, cross)


def swap(value, axis):
    return lax.ppermute(value, axis, [(0, 1), (1, 0)])


def shift(value):
    n = lax.axis_size("patch")
    return lax.ppermute(value, "patch", [(i, (i + 1) % n) for i in range(n)])


def paired(patches, dictionary, threshold):
    n_patch = lax.axis_size("patch")
    plane = lax.axis_index("patch")
    core = lax.axis_index("atom")
    half = lax.axis_index("feat")
    rows = patches.shape[0]
    count = rows * n_patch
    block = dictionary.shape[1] // 2
    step = rows // CHUNKS
    f32 = jnp.float32

    values = patches.astype(f32)
    local_sq = jnp.sum(values * values, axis=1)
    energy = local_sq + swap(local_sq, "feat")
    scale = lax.rsqrt(energy[:, None] / (BINS * VOXELS) + 1e-05)
    normed = (scale * values).astype(jnp.bfloat16)
    normed_of = [normed]
    level = step_rate * threshold[None, :]
    mine = half * block
    theirs = (1 - half) * block
    keep = lax.dynamic_slice_in_dim(dictionary, mine, block, 1)
    send = lax.dynamic_slice_in_dim(dictionary, theirs, block, 1)
    level_keep = lax.dynamic_slice_in_dim(level, mine, block, 1)

    parts = []
    for c in range(CHUNKS):
        part = jnp.dot(patches[c * step : (c + 1) * step], dictionary, preferred_element_type=f32)
        part = part.astype(jnp.bfloat16)
        parts.append((part, swap(part, "feat")))
    for k in range(1, n_patch):
        normed_of.append(shift(normed_of[-1]))
    codes_of = []
    for c in range(CHUNKS):
        window = slice(c * step, (c + 1) * step)
        part, other = parts[c]
        summed = part.astype(f32) + other.astype(f32)
        start = soften(step_rate * (scale[window] * summed), level).astype(jnp.bfloat16)
        own = lax.dot_general(start, dictionary, (((1,), (1,)), ((), ())), preferred_element_type=f32)
        rebuilt = own + swap(own, "atom")
        misfit = (scale[window] * values[window] - rebuilt).astype(jnp.bfloat16)
        away = jnp.dot(misfit, send, preferred_element_type=f32).astype(jnp.bfloat16)
        arrived = swap(away, "feat")
        second = jnp.dot(misfit, keep, preferred_element_type=f32) + arrived.astype(f32)
        start_keep = lax.dynamic_slice_in_dim(start, mine, block, 1).astype(f32)
        codes_of.append(soften(start_keep + step_rate * second, level_keep).astype(jnp.bfloat16))

    left = [codes_of]
    for k in range(1, n_patch):
        left.append([shift(x) for x in left[-1]])
    outside = [swap(x, "feat") for x in codes_of]
    own_rows = jnp.concatenate(codes_of, 0)
    other_rows = jnp.concatenate(outside, 0)
    codes = jnp.where(
        half == 0,
        jnp.concatenate([own_rows, other_rows], 1),
        jnp.concatenate([other_rows, own_rows], 1),
    )
    home_core = plane // 2
    home_half = plane % 2
    over = [((q * 2 + q // 2) * 2 + q % 2, (q * 2 + q // 2) * 2 + 1 - q % 2) for q in range(n_patch)]
    across = [(q * 2 + q // 2, q * 2 + 1 - q // 2) for q in range(n_patch)]
    first = (((0,), (0,)), ((), ()))
    gram = 0.0
    cross = 0.0
    for k in range(n_patch):
        for c in range(CHUNKS):
            lhs = left[k][c]
            if k == 0:
                there = jnp.where(half == home_half, lhs, outside[c])
            else:
                there = jnp.where(
                    half == home_half, lhs, lax.ppermute(lhs, ("patch", "atom", "feat"), over)
                )
            rhs = jnp.where(core == home_core, there, lax.ppermute(there, ("patch", "atom"), across))
            gram += lax.dot_general(lhs, rhs, first, preferred_element_type=f32)
            narrow = lax.dynamic_slice_in_dim(rhs, core * (block // 2), block // 2, 1)
            cross += lax.dot_general(
                normed_of[k][c * step : (c + 1) * step], narrow, first, preferred_element_type=f32
            )
    return (codes, gram / count, cross / count)


def solution(mesh):
    in_specs = (P(("slab", "patch"), "feat"), P("feat", "atom"), P("atom"))
    out_specs = (
        P(("slab", "patch"), "atom"),
        P(("slab", "atom", "feat"), "patch"),
        P(("slab", "feat"), ("patch", "atom")),
    )
    sizes = mesh.shape
    small = sizes["feat"] == 2 and sizes["atom"] == 2 and sizes["patch"] == 4
    return jax.shard_map(
        paired if small else general, mesh=mesh, in_specs=in_specs, out_specs=out_specs, check_vma=False
    )
```

```python
import jax
import jax.numpy as jnp
from jax import lax
from jax.sharding import PartitionSpec as P

BINS = 8
VOXELS = 216


step_rate = 0.2
CHUNKS = 2


def soften(value, level):
    return jnp.sign(value) * jnp.maximum(jnp.abs(value) - level, 0.0)


def general(patches, dictionary, threshold):
    values = patches.astype(jnp.float32)
    local_sq = jnp.sum(values * values, axis=1)
    local_first = jnp.dot(patches, dictionary, preferred_element_type=jnp.float32)
    summed, energy = lax.psum((local_first, local_sq), "feat")
    scale = lax.rsqrt(energy[:, None] / (BINS * VOXELS) + 1e-05)
    level = step_rate * threshold[None, :]
    start = soften(step_rate * (scale * summed), level).astype(jnp.bfloat16)
    contract_last = (((1,), (1,)), ((), ()))
    own_part = lax.dot_general(start, dictionary, contract_last, preferred_element_type=jnp.float32)
    rebuilt = lax.psum(own_part, "atom")
    misfit = (scale * values - rebuilt).astype(jnp.bfloat16)
    local_second = jnp.dot(misfit, dictionary, preferred_element_type=jnp.float32)
    second = lax.psum(local_second, "feat")
    codes = soften(start.astype(jnp.float32) + step_rate * second, level).astype(jnp.bfloat16)
    codes_whole = lax.all_gather(codes, "atom", axis=1, tiled=True)
    n_patch = lax.axis_size("patch")
    n_atom = lax.axis_size("atom")
    n_feat = lax.axis_size("feat")
    total_atoms = codes_whole.shape[1]
    count = patches.shape[0] * n_patch
    contract_first = (((0,), (0,)), ((), ()))
    block_rows = total_atoms // (n_atom * n_feat)
    offset = (lax.axis_index("atom") * n_feat + lax.axis_index("feat")) * block_rows
    chosen = lax.dynamic_slice_in_dim(codes_whole, offset, block_rows, 1)
    gram_part = lax.dot_general(
        chosen, codes_whole, contract_first, preferred_element_type=jnp.float32
    )
    gram = (
        lax.psum_scatter(
            gram_part.astype(jnp.bfloat16), "patch", scatter_dimension=1, tiled=True
        ).astype(jnp.float32)
        / count
    )
    width = total_atoms // (n_patch * n_atom)
    arranged = codes_whole.reshape(codes_whole.shape[0], n_patch, n_atom, width)
    picked = lax.dynamic_slice_in_dim(arranged, lax.axis_index("atom"), 1, 2).reshape(
        codes_whole.shape[0], n_patch * width
    )
    normed = (scale * values).astype(jnp.bfloat16)
    cross_part = lax.dot_general(normed, picked, contract_first, preferred_element_type=jnp.float32)
    cross = (
        lax.psum_scatter(
            cross_part.astype(jnp.bfloat16), "patch", scatter_dimension=1, tiled=True
        ).astype(jnp.float32)
        / count
    )
    return (codes, gram, cross)


def swap(value, axis):
    return lax.ppermute(value, axis, [(0, 1), (1, 0)])


def shift(value):
    n = lax.axis_size("patch")
    return lax.ppermute(value, "patch", [(i, (i + 1) % n) for i in range(n)])


def after(value, earlier):
    return lax.optimization_barrier((value, earlier))[0]


def paired(patches, dictionary, threshold):
    n_patch = lax.axis_size("patch")
    plane = lax.axis_index("patch")
    core = lax.axis_index("atom")
    half = lax.axis_index("feat")
    count = patches.shape[0] * n_patch
    rows = patches.shape[0] // 2
    block = dictionary.shape[1] // 2
    step = rows // CHUNKS
    f32, bf16 = jnp.float32, jnp.bfloat16
    last = (((1,), (1,)), ((), ()))
    first = (((0,), (0,)), ((), ()))

    def blocks(array, which):
        return lax.dynamic_slice_in_dim(array, which * block, block, 1)

    dictionary2 = swap(dictionary, "atom")
    level = step_rate * threshold[None, :]
    level2 = swap(level, "atom")
    mine = lax.dynamic_slice_in_dim(patches, core * rows, rows, 0)
    part = jnp.dot(mine, dictionary, preferred_element_type=f32).astype(bf16)
    other = swap(part, "feat")
    values = mine.astype(f32)
    local_sq = jnp.sum(values * values, axis=1)
    energy = local_sq + swap(local_sq, "feat")
    scale = lax.rsqrt(energy[:, None] / (BINS * VOXELS) + 1e-05)
    normed = (scale * values).astype(bf16)
    part2, other2 = [], []
    for c in range(CHUNKS):
        window = slice(c * step, (c + 1) * step)
        part2.append(jnp.dot(mine[window], dictionary2, preferred_element_type=f32).astype(bf16))
        other2.append(swap(part2[c], "feat"))
    start = soften(step_rate * (scale * (part.astype(f32) + other.astype(f32))), level).astype(bf16)
    built = lax.dot_general(start, dictionary, last, preferred_element_type=f32)
    normed_of = [normed]
    for k in range(1, n_patch):
        normed_of.append(shift(normed_of[-1]))

    codes_of = []
    done = built
    for c in range(CHUNKS):
        window = slice(c * step, (c + 1) * step)
        arrived = after(other2[c], done).astype(f32)
        start2 = soften(step_rate * (scale[window] * (part2[c].astype(f32) + arrived)), level2).astype(bf16)
        rebuilt = built[window] + lax.dot_general(start2, dictionary2, last, preferred_element_type=f32)
        misfit = (scale[window] * values[window] - rebuilt).astype(bf16)
        away = jnp.concatenate(
            [
                jnp.dot(misfit, blocks(d, 1 - half), preferred_element_type=f32).astype(bf16)
                for d in (dictionary, dictionary2)
            ],
            1,
        )
        done = away
        back = swap(away, "feat").astype(f32)
        pieces = []
        for i, (d, s, t) in enumerate(((dictionary, start[window], level), (dictionary2, start2, level2))):
            second = jnp.dot(misfit, blocks(d, half), preferred_element_type=f32)
            second += back[:, i * block : (i + 1) * block]
            pieces.append(soften(blocks(s, half).astype(f32) + step_rate * second, blocks(t, half)).astype(bf16))
        codes_of.append(jnp.concatenate(pieces, 1))

    left = [codes_of]
    for k in range(1, n_patch):
        left.append([shift(x) for x in left[-1]])
    left = [jnp.concatenate(x, 0) for x in left]
    inside = left[0]
    outside = swap(inside, "feat")
    both = [jnp.where(half == 0, inside, outside), jnp.where(half == 0, outside, inside)]
    upper = jnp.concatenate([x[:, :block] for x in both], 1)
    lower = swap(jnp.concatenate([x[:, block:] for x in both], 1), "atom")
    codes = jnp.where(
        core == 0, jnp.concatenate([upper, lower], 0), jnp.concatenate([lower, upper], 0)
    )
    home_core = plane // 2
    home_half = plane % 2
    place = jnp.where(core == home_core, 0, 1)
    over = [(q * 2 + q % 2, q * 2 + 1 - q % 2) for q in range(n_patch)]
    products = 0.0
    for k in range(n_patch):
        here = blocks(left[k], place)
        there = blocks(outside, place) if k == 0 else lax.ppermute(here, ("patch", "feat"), over)
        right = jnp.where(half == home_half, here, there)
        sides = jnp.concatenate([left[k], normed_of[k]], 1)
        products += lax.dot_general(sides, right, first, preferred_element_type=f32)
    width = block // 2
    gram = products[:block] + swap(products[block : 2 * block], "atom")
    cross = lax.dynamic_slice_in_dim(products[2 * block :], core * width, width, 1) + swap(
        lax.dynamic_slice_in_dim(products[2 * block :], (1 - core) * width, width, 1), "atom"
    )
    return (codes, gram / count, cross / count)


def solution(mesh):
    in_specs = (P(("slab", "patch"), "feat"), P("feat", "atom"), P("atom"))
    out_specs = (
        P(("slab", "patch"), "atom"),
        P(("slab", "atom", "feat"), "patch"),
        P(("slab", "feat"), ("patch", "atom")),
    )
    sizes = mesh.shape
    small = sizes["feat"] == 2 and sizes["atom"] == 2 and sizes["patch"] == 4
    return jax.shard_map(
        paired if small else general, mesh=mesh, in_specs=in_specs, out_specs=out_specs, check_vma=False
    )
```

```python
import jax
import jax.numpy as jnp
from jax import lax
from jax.sharding import PartitionSpec as P

BINS = 8
VOXELS = 216


step_rate = 0.2
CHUNKS = 2


def soften(value, level):
    return jnp.sign(value) * jnp.maximum(jnp.abs(value) - level, 0.0)


def general(patches, dictionary, threshold):
    values = patches.astype(jnp.float32)
    local_sq = jnp.sum(values * values, axis=1)
    local_first = jnp.dot(patches, dictionary, preferred_element_type=jnp.float32)
    summed, energy = lax.psum((local_first, local_sq), "feat")
    scale = lax.rsqrt(energy[:, None] / (BINS * VOXELS) + 1e-05)
    level = step_rate * threshold[None, :]
    start = soften(step_rate * (scale * summed), level).astype(jnp.bfloat16)
    contract_last = (((1,), (1,)), ((), ()))
    own_part = lax.dot_general(start, dictionary, contract_last, preferred_element_type=jnp.float32)
    rebuilt = lax.psum(own_part, "atom")
    misfit = (scale * values - rebuilt).astype(jnp.bfloat16)
    local_second = jnp.dot(misfit, dictionary, preferred_element_type=jnp.float32)
    second = lax.psum(local_second, "feat")
    codes = soften(start.astype(jnp.float32) + step_rate * second, level).astype(jnp.bfloat16)
    codes_whole = lax.all_gather(codes, "atom", axis=1, tiled=True)
    n_patch = lax.axis_size("patch")
    n_atom = lax.axis_size("atom")
    n_feat = lax.axis_size("feat")
    total_atoms = codes_whole.shape[1]
    count = patches.shape[0] * n_patch
    contract_first = (((0,), (0,)), ((), ()))
    block_rows = total_atoms // (n_atom * n_feat)
    offset = (lax.axis_index("atom") * n_feat + lax.axis_index("feat")) * block_rows
    chosen = lax.dynamic_slice_in_dim(codes_whole, offset, block_rows, 1)
    gram_part = lax.dot_general(
        chosen, codes_whole, contract_first, preferred_element_type=jnp.float32
    )
    gram = (
        lax.psum_scatter(
            gram_part.astype(jnp.bfloat16), "patch", scatter_dimension=1, tiled=True
        ).astype(jnp.float32)
        / count
    )
    width = total_atoms // (n_patch * n_atom)
    arranged = codes_whole.reshape(codes_whole.shape[0], n_patch, n_atom, width)
    picked = lax.dynamic_slice_in_dim(arranged, lax.axis_index("atom"), 1, 2).reshape(
        codes_whole.shape[0], n_patch * width
    )
    normed = (scale * values).astype(jnp.bfloat16)
    cross_part = lax.dot_general(normed, picked, contract_first, preferred_element_type=jnp.float32)
    cross = (
        lax.psum_scatter(
            cross_part.astype(jnp.bfloat16), "patch", scatter_dimension=1, tiled=True
        ).astype(jnp.float32)
        / count
    )
    return (codes, gram, cross)


def swap(value, axis):
    return lax.ppermute(value, axis, [(0, 1), (1, 0)])


def shift(value):
    n = lax.axis_size("patch")
    return lax.ppermute(value, "patch", [(i, (i + 1) % n) for i in range(n)])


def after(value, earlier):
    return lax.optimization_barrier((value, earlier))[0]


def paired(patches, dictionary, threshold):
    n_patch = lax.axis_size("patch")
    plane = lax.axis_index("patch")
    core = lax.axis_index("atom")
    half = lax.axis_index("feat")
    count = patches.shape[0] * n_patch
    rows = patches.shape[0] // 2
    atoms = dictionary.shape[1]
    block = atoms // 2
    step = rows // CHUNKS
    f32, bf16 = jnp.float32, jnp.bfloat16
    last = (((1,), (1,)), ((), ()))
    first = (((0,), (0,)), ((), ()))

    def blocks(array, which):
        return lax.dynamic_slice_in_dim(array, which * block, block, 1)

    mine = lax.dynamic_slice_in_dim(patches, core * rows, rows, 0)
    values = mine.astype(f32)
    local_sq = jnp.sum(values * values, axis=1)
    other_sq = swap(local_sq, "feat")
    dictionary2 = swap(dictionary, "atom")
    windows = [slice(c * step, (c + 1) * step) for c in range(CHUNKS)]
    parts = []
    for w in windows:
        parts.append([jnp.dot(mine[w], d, preferred_element_type=f32).astype(bf16) for d in (dictionary, dictionary2)])
    others = [swap(jnp.concatenate(p, 1), "feat") for p in parts]
    level = step_rate * threshold[None, :]
    level2 = swap(level, "atom")
    energy = local_sq + after(other_sq, parts)
    scale = lax.rsqrt(energy[:, None] / (BINS * VOXELS) + 1e-05)
    normed = (scale * values).astype(bf16)
    normed_of = [normed, shift(normed)]

    starts, backs, kept = [], [], []
    done = normed
    for c, w in enumerate(windows):
        other = after(others[c], done).astype(f32)
        start = []
        for i, t in enumerate((level, level2)):
            summed = parts[c][i].astype(f32) + other[:, i * atoms : (i + 1) * atoms]
            start.append(soften(step_rate * (scale[w] * summed), t).astype(bf16))
        rebuilt = lax.dot_general(start[0], dictionary, last, preferred_element_type=f32)
        rebuilt += lax.dot_general(start[1], dictionary2, last, preferred_element_type=f32)
        misfit = (scale[w] * values[w] - rebuilt).astype(bf16)
        away = [
            jnp.dot(misfit, blocks(d, 1 - half), preferred_element_type=f32).astype(bf16)
            for d in (dictionary, dictionary2)
        ]
        done = away
        starts.append(start)
        backs.append(swap(jnp.concatenate(away, 1), "feat"))
        kept.append(
            [jnp.dot(misfit, blocks(d, half), preferred_element_type=f32) for d in (dictionary, dictionary2)]
        )
        normed_of.append(shift(after(normed_of[-1], away)))

    codes_of = []
    for c, w in enumerate(windows):
        back = after(backs[c], done).astype(f32)
        pieces = []
        for i, t in enumerate((level, level2)):
            second = kept[c][i] + back[:, i * block : (i + 1) * block]
            base = blocks(starts[c][i], half).astype(f32)
            pieces.append(soften(base + step_rate * second, blocks(t, half)).astype(bf16))
        codes_of.append(jnp.concatenate(pieces, 1))
        done = codes_of[c]

    rings = [codes_of]
    for k in range(1, n_patch):
        rings.append([shift(x) for x in rings[-1]])
    left = [jnp.concatenate(x, 0) for x in rings]
    inside = left[0]
    outside = swap(inside, "feat")

    home_core = plane // 2
    home_half = plane % 2
    place = jnp.where(core == home_core, 0, 1)
    here = [blocks(x, place) for x in left]
    over = [(q * 2 + q % 2, q * 2 + 1 - q % 2) for q in range(n_patch)]
    middle = lax.ppermute(jnp.concatenate(here[1:-1], 0), ("patch", "feat"), over)
    below = (plane + n_patch - 1) % n_patch
    place_below = jnp.where(core == below // 2, 0, 1)
    down = [
        (q * 2 + 1 - (q - 1) % n_patch % 2, (q - 1) % n_patch * 2 + 1 - (q - 1) % n_patch % 2) for q in range(n_patch)
    ]
    final = lax.ppermute(blocks(outside, place_below), ("patch", "feat"), down)
    there = [blocks(outside, place), middle[:rows], middle[rows:], final]
    right = [jnp.where(half == home_half, h, t) for h, t in zip(here, there)]

    both = [jnp.where(half == 0, inside, outside), jnp.where(half == 0, outside, inside)]
    upper = jnp.concatenate([x[:, :block] for x in both], 1)
    lower = after(jnp.concatenate([x[:, block:] for x in both], 1), rings[1])
    lower = after(swap(lower, "atom"), rings[2])
    codes = jnp.where(
        core == 0, jnp.concatenate([upper, lower], 0), jnp.concatenate([lower, upper], 0)
    )

    gram_part = 0.0
    cross_part = 0.0
    for k in range(n_patch):
        gram_part += lax.dot_general(left[k], right[k], first, preferred_element_type=f32)
        cross_part += lax.dot_general(normed_of[k], right[k], first, preferred_element_type=f32)
        if k == n_patch - 2:
            gram_part, cross_part, codes = lax.optimization_barrier((gram_part, cross_part, codes))
    width = block // 2
    gram = gram_part[:block] + swap(gram_part[block:].astype(bf16), "atom").astype(f32)
    cross = lax.dynamic_slice_in_dim(cross_part, core * width, width, 1)
    cross += swap(
        lax.dynamic_slice_in_dim(cross_part, (1 - core) * width, width, 1).astype(bf16), "atom"
    ).astype(f32)
    return (codes, gram / count, cross / count)


def solution(mesh):
    in_specs = (P(("slab", "patch"), "feat"), P("feat", "atom"), P("atom"))
    out_specs = (
        P(("slab", "patch"), "atom"),
        P(("slab", "atom", "feat"), "patch"),
        P(("slab", "feat"), ("patch", "atom")),
    )
    sizes = mesh.shape
    small = sizes["feat"] == 2 and sizes["atom"] == 2 and sizes["patch"] == 4
    return jax.shard_map(
        paired if small else general, mesh=mesh, in_specs=in_specs, out_specs=out_specs, check_vma=False
    )
```

```python
import jax
import jax.numpy as jnp
from jax import lax
from jax.sharding import PartitionSpec as P

BINS = 8
VOXELS = 216


step_rate = 0.2
CHUNKS = 2


def soften(value, level):
    return jnp.sign(value) * jnp.maximum(jnp.abs(value) - level, 0.0)


def general(patches, dictionary, threshold):
    values = patches.astype(jnp.float32)
    local_sq = jnp.sum(values * values, axis=1)
    local_first = jnp.dot(patches, dictionary, preferred_element_type=jnp.float32)
    summed, energy = lax.psum((local_first, local_sq), "feat")
    scale = lax.rsqrt(energy[:, None] / (BINS * VOXELS) + 1e-05)
    level = step_rate * threshold[None, :]
    start = soften(step_rate * (scale * summed), level).astype(jnp.bfloat16)
    contract_last = (((1,), (1,)), ((), ()))
    own_part = lax.dot_general(start, dictionary, contract_last, preferred_element_type=jnp.float32)
    rebuilt = lax.psum(own_part, "atom")
    misfit = (scale * values - rebuilt).astype(jnp.bfloat16)
    local_second = jnp.dot(misfit, dictionary, preferred_element_type=jnp.float32)
    second = lax.psum(local_second, "feat")
    codes = soften(start.astype(jnp.float32) + step_rate * second, level).astype(jnp.bfloat16)
    codes_whole = lax.all_gather(codes, "atom", axis=1, tiled=True)
    n_patch = lax.axis_size("patch")
    n_atom = lax.axis_size("atom")
    n_feat = lax.axis_size("feat")
    total_atoms = codes_whole.shape[1]
    count = patches.shape[0] * n_patch
    contract_first = (((0,), (0,)), ((), ()))
    block_rows = total_atoms // (n_atom * n_feat)
    offset = (lax.axis_index("atom") * n_feat + lax.axis_index("feat")) * block_rows
    chosen = lax.dynamic_slice_in_dim(codes_whole, offset, block_rows, 1)
    gram_part = lax.dot_general(
        chosen, codes_whole, contract_first, preferred_element_type=jnp.float32
    )
    gram = (
        lax.psum_scatter(
            gram_part.astype(jnp.bfloat16), "patch", scatter_dimension=1, tiled=True
        ).astype(jnp.float32)
        / count
    )
    width = total_atoms // (n_patch * n_atom)
    arranged = codes_whole.reshape(codes_whole.shape[0], n_patch, n_atom, width)
    picked = lax.dynamic_slice_in_dim(arranged, lax.axis_index("atom"), 1, 2).reshape(
        codes_whole.shape[0], n_patch * width
    )
    normed = (scale * values).astype(jnp.bfloat16)
    cross_part = lax.dot_general(normed, picked, contract_first, preferred_element_type=jnp.float32)
    cross = (
        lax.psum_scatter(
            cross_part.astype(jnp.bfloat16), "patch", scatter_dimension=1, tiled=True
        ).astype(jnp.float32)
        / count
    )
    return (codes, gram, cross)


def swap(value, axis):
    return lax.ppermute(value, axis, [(0, 1), (1, 0)])


def shift(value):
    n = lax.axis_size("patch")
    return lax.ppermute(value, "patch", [(i, (i + 1) % n) for i in range(n)])


def after(value, earlier):
    return lax.optimization_barrier((value, earlier))[0]


def paired(patches, dictionary, threshold):
    n_patch = lax.axis_size("patch")
    plane = lax.axis_index("patch")
    core = lax.axis_index("atom")
    half = lax.axis_index("feat")
    count = patches.shape[0] * n_patch
    rows = patches.shape[0] // 2
    atoms = dictionary.shape[1]
    block = atoms // 2
    width = block // 2
    step = rows // CHUNKS
    f32, bf16 = jnp.float32, jnp.bfloat16
    last = (((1,), (1,)), ((), ()))
    first = (((0,), (0,)), ((), ()))

    def blocks(array, which, size=block):
        return lax.dynamic_slice_in_dim(array, which * size, size, 1)

    def group(own, other, which):
        return jnp.concatenate([blocks(own, which), blocks(other, which)], 1)

    def times(a, b):
        return jnp.dot(a, b, preferred_element_type=f32)

    mine = lax.dynamic_slice_in_dim(patches, core * rows, rows, 0)
    values = mine.astype(f32)
    local_sq = jnp.sum(values * values, axis=1)
    other_sq = swap(local_sq, "feat")
    dictionary2 = swap(dictionary, "atom")
    near = group(dictionary, dictionary2, half)
    far = group(dictionary, dictionary2, 1 - half)
    windows = [slice(c * step, (c + 1) * step) for c in range(CHUNKS)]
    parts, others = [], []
    done = ()
    for w in windows:
        piece = after(mine[w], done)
        parts.append([times(piece, d).astype(bf16) for d in (near, far)])
        done = parts[-1]
        others.append(swap(jnp.concatenate(parts[-1], 1), "feat"))
    level = step_rate * threshold[None, :]
    level2 = swap(after(level, done), "atom")
    levels = [group(level, level2, half), group(level, level2, 1 - half)]
    energy = local_sq + after(other_sq, done)
    scale = lax.rsqrt(energy[:, None] / (BINS * VOXELS) + 1e-05)
    normed = (scale * values).astype(bf16)
    normed_of = [normed, shift(normed)]

    base, backs = [], []
    done = normed_of
    for c, w in enumerate(windows):
        other = after(others[c], done).astype(f32)
        summed = [parts[c][0].astype(f32) + other[:, atoms:], parts[c][1].astype(f32) + other[:, :atoms]]
        start = [soften(step_rate * (scale[w] * x), t).astype(bf16) for x, t in zip(summed, levels)]
        rebuilt = sum(
            lax.dot_general(x, d, last, preferred_element_type=f32) for x, d in zip(start, (near, far))
        )
        misfit = (scale[w] * values[w] - rebuilt).astype(bf16)
        backs.append(swap(times(misfit, far).astype(bf16), "feat"))
        base.append(start[0].astype(f32) + step_rate * times(misfit, near))
        normed_of.append(shift(after(normed_of[-1], start)))
        done = (backs[-1], normed_of[-1]) if c == 0 else (misfit,)

    codes_of = []
    for c, w in enumerate(windows):
        back = after(backs[c], done).astype(f32)
        codes_of.append(soften(base[c] + step_rate * back, levels[0]).astype(bf16))
        done = codes_of[c]

    rings = [codes_of]
    for k in range(1, n_patch):
        rings.append([shift(x) for x in rings[-1]])
    left = [jnp.concatenate(x, 0) for x in rings]
    inside = left[0]
    outside = swap(inside, "feat")

    home_half = plane % 2
    place = jnp.where(core == plane // 2, 0, 1)
    here = [blocks(x, place) for x in left]
    over = [(q * 2 + q % 2, q * 2 + 1 - q % 2) for q in range(n_patch)]
    below = (plane + n_patch - 1) % n_patch
    place_below = jnp.where(core == below // 2, 0, 1)
    down = [
        (q * 2 + 1 - (q - 1) % n_patch % 2, (q - 1) % n_patch * 2 + 1 - (q - 1) % n_patch % 2) for q in range(n_patch)
    ]
    there = [blocks(outside, place)]
    for k in range(1, n_patch - 1):
        there.append(lax.ppermute(here[k], ("patch", "feat"), over))
    there.append(lax.ppermute(blocks(outside, place_below), ("patch", "feat"), down))
    right = [jnp.where(half == home_half, h, t) for h, t in zip(here, there)]

    both = [jnp.where(half == 0, inside, outside), jnp.where(half == 0, outside, inside)]
    upper = jnp.concatenate([x[:, :block] for x in both], 1)
    lower = swap(jnp.concatenate([x[:, block:] for x in both], 1), "atom")
    lower = after(lower, rings[1])
    codes = jnp.where(
        core == 0, jnp.concatenate([upper, lower], 0), jnp.concatenate([lower, upper], 0)
    )

    def product(lhs, rhs):
        return lax.dot_general(lhs, rhs, first, preferred_element_type=f32)

    steps = range(n_patch - 1)
    gram_send = sum(product(left[k][:, block:], right[k]) for k in steps).astype(bf16)
    cross_send = sum(product(normed_of[k], blocks(right[k], 1 - core, width)) for k in steps).astype(bf16)
    gram = sum(product(left[k][:, :block], right[k]) for k in steps)
    cross = sum(product(normed_of[k], blocks(right[k], core, width)) for k in steps)
    gram += swap(gram_send, "atom").astype(f32)
    cross += swap(cross_send, "atom").astype(f32)
    late = jnp.concatenate([rings[-1][-1][:, block:], right[-1][-step:]], 1)
    early = jnp.concatenate([rings[-1][0][:, block:], right[-1][:-step]], 1)
    early = swap(early, "atom")
    normed_last = swap(after(normed_of[-1], rings[1]), "atom")
    codes, gram, cross, late, normed_last = lax.optimization_barrier((codes, gram, cross, late, normed_last))
    late = swap(late, "atom")
    gram += product(left[-1][:, :block], right[-1])
    cross += product(normed_of[-1], blocks(right[-1], core, width))
    for c, x in enumerate((early, late)):
        gram += product(x[:, :block], x[:, block:])
        cross += product(normed_last[windows[c]], blocks(x[:, block:], core, width))
    return (codes, gram / count, cross / count)


def solution(mesh):
    in_specs = (P(("slab", "patch"), "feat"), P("feat", "atom"), P("atom"))
    out_specs = (
        P(("slab", "patch"), "atom"),
        P(("slab", "atom", "feat"), "patch"),
        P(("slab", "feat"), ("patch", "atom")),
    )
    sizes = mesh.shape
    small = sizes["feat"] == 2 and sizes["atom"] == 2 and sizes["patch"] == 4
    return jax.shard_map(
        paired if small else general, mesh=mesh, in_specs=in_specs, out_specs=out_specs, check_vma=False
    )
```

```python
import functools

import jax
import jax.numpy as jnp
from jax import lax
from jax.experimental import pallas as pl
from jax.experimental.pallas import tpu as pltpu
from jax.sharding import PartitionSpec as P

BINS = 8
VOXELS = 216


step_rate = 0.2


def soften(value, level):
    return jnp.sign(value) * jnp.maximum(jnp.abs(value) - level, 0.0)


def general(patches, dictionary, threshold):
    values = patches.astype(jnp.float32)
    local_sq = jnp.sum(values * values, axis=1)
    local_first = jnp.dot(patches, dictionary, preferred_element_type=jnp.float32)
    summed, energy = lax.psum((local_first, local_sq), "feat")
    scale = lax.rsqrt(energy[:, None] / (BINS * VOXELS) + 1e-05)
    level = step_rate * threshold[None, :]
    start = soften(step_rate * (scale * summed), level).astype(jnp.bfloat16)
    contract_last = (((1,), (1,)), ((), ()))
    own_part = lax.dot_general(start, dictionary, contract_last, preferred_element_type=jnp.float32)
    rebuilt = lax.psum(own_part, "atom")
    misfit = (scale * values - rebuilt).astype(jnp.bfloat16)
    local_second = jnp.dot(misfit, dictionary, preferred_element_type=jnp.float32)
    second = lax.psum(local_second, "feat")
    codes = soften(start.astype(jnp.float32) + step_rate * second, level).astype(jnp.bfloat16)
    codes_whole = lax.all_gather(codes, "atom", axis=1, tiled=True)
    n_patch = lax.axis_size("patch")
    n_atom = lax.axis_size("atom")
    n_feat = lax.axis_size("feat")
    total_atoms = codes_whole.shape[1]
    count = patches.shape[0] * n_patch
    contract_first = (((0,), (0,)), ((), ()))
    block_rows = total_atoms // (n_atom * n_feat)
    offset = (lax.axis_index("atom") * n_feat + lax.axis_index("feat")) * block_rows
    chosen = lax.dynamic_slice_in_dim(codes_whole, offset, block_rows, 1)
    gram_part = lax.dot_general(
        chosen, codes_whole, contract_first, preferred_element_type=jnp.float32
    )
    gram = (
        lax.psum_scatter(
            gram_part.astype(jnp.bfloat16), "patch", scatter_dimension=1, tiled=True
        ).astype(jnp.float32)
        / count
    )
    width = total_atoms // (n_patch * n_atom)
    arranged = codes_whole.reshape(codes_whole.shape[0], n_patch, n_atom, width)
    picked = lax.dynamic_slice_in_dim(arranged, lax.axis_index("atom"), 1, 2).reshape(
        codes_whole.shape[0], n_patch * width
    )
    normed = (scale * values).astype(jnp.bfloat16)
    cross_part = lax.dot_general(normed, picked, contract_first, preferred_element_type=jnp.float32)
    cross = (
        lax.psum_scatter(
            cross_part.astype(jnp.bfloat16), "patch", scatter_dimension=1, tiled=True
        ).astype(jnp.float32)
        / count
    )
    return (codes, gram, cross)


def swap(value, axis):
    return lax.ppermute(value, axis, [(0, 1), (1, 0)])


def shift(value):
    n = lax.axis_size("patch")
    return lax.ppermute(value, "patch", [(i, (i + 1) % n) for i in range(n)])


def after(value, earlier):
    return lax.optimization_barrier((value, earlier))[0]


f32, bf16 = jnp.float32, jnp.bfloat16
contract_last = (((1,), (1,)), ((), ()))
contract_first = (((0,), (0,)), ((), ()))


def soft(value, level):
    return jnp.where(value > level, value - level, jnp.where(value < -level, value + level, 0.0))


def run(body, outs, scalars, arrays, scratch=()):
    fast = pl.BlockSpec(memory_space=pltpu.VMEM)
    slow = pl.BlockSpec(memory_space=pltpu.SMEM)
    return pl.pallas_call(
        body,
        out_shape=outs,
        in_specs=[slow] + [fast] * len(arrays),
        out_specs=jax.tree.map(lambda _: fast, outs),
        scratch_shapes=scratch,
        compiler_params=pltpu.CompilerParams(vmem_limit_bytes=24 << 20),
        cost_estimate=pl.CostEstimate(flops=1000, bytes_accessed=1000, transcendentals=0),
    )(jnp.stack([x.astype(jnp.int32) for x in scalars]), *arrays)


def first_body(_, mine, own, other, out):
    atoms = own.shape[1]
    for i, d in enumerate((own, other)):
        out[:, i * atoms : (i + 1) * atoms] = jnp.dot(mine[...], d[...], preferred_element_type=f32).astype(bf16)


def second_body(where, part, arrived, mine, scale, threshold, own, other, away, base, start):
    atoms = own.shape[1]
    block = atoms // 2
    near = pl.multiple_of(where[0] * block, block)
    far = pl.multiple_of((1 - where[0]) * block, block)
    factor = scale[...]
    summed = part[...].astype(f32) + arrived[...].astype(f32)
    start[...] = soft(step_rate * (factor * summed), step_rate * threshold[...]).astype(bf16)
    rebuilt = sum(
        lax.dot_general(start[:, i * atoms : (i + 1) * atoms], d[...], contract_last, preferred_element_type=f32)
        for i, d in enumerate((own, other))
    )
    misfit = (factor * mine[...].astype(f32) - rebuilt).astype(bf16)
    for i, d in enumerate((own, other)):
        columns = slice(i * block, (i + 1) * block)
        away[:, columns] = jnp.dot(misfit, d[:, pl.ds(far, block)], preferred_element_type=f32).astype(bf16)
    for i, d in enumerate((own, other)):
        columns = slice(i * block, (i + 1) * block)
        second = jnp.dot(misfit, d[:, pl.ds(near, block)], preferred_element_type=f32)
        base[:, columns] = start[:, pl.ds(pl.multiple_of(i * atoms + near, block), block)].astype(f32) + (
            step_rate * second
        )


def sums_body(n, where, *refs):
    pieces, (gram, cross, send, lhs, sides, right) = refs[:-6], refs[-6:]
    block = right.shape[1]
    width = block // 2
    place = pl.multiple_of(where[0] * block, block)
    here = where[1] == 1
    rows = lhs.shape[0] // n
    for k in range(n):
        chunks, (there, raw, scale) = pieces[k * 5 : k * 5 + 2], pieces[k * 5 + 2 : k * 5 + 5]
        step = rows // 2
        for c, x in enumerate(chunks):
            window = slice(k * rows + c * step, k * rows + (c + 1) * step)
            lhs[window, :] = x[...]
            spot = pl.multiple_of(where[3 + k] * block, block)
            right[window, :] = jnp.where(
                here, x[:, pl.ds(place, block)], there[c * step : (c + 1) * step, pl.ds(spot, block)]
            )
        sides[k * rows : (k + 1) * rows, :] = (scale[...] * raw[...].astype(f32)).astype(bf16)
    mine = pl.multiple_of(where[2] * width, width)
    theirs = pl.multiple_of((1 - where[2]) * width, width)

    def product(a, b):
        return lax.dot_general(a, b, contract_first, preferred_element_type=f32)

    send[:block, :] = product(lhs[:, block:], right[...]).astype(bf16)
    part = product(sides[...], right[:, pl.ds(theirs, width)]).astype(bf16)
    tall = part.shape[0] // 2
    send[block:, :width] = part[:tall]
    send[block:, width:] = part[tall:]
    gram[...] = product(lhs[:, :block], right[...])
    cross[...] = product(sides[...], right[:, pl.ds(mine, width)])


def last_body(count, where, *refs):
    gram_in, cross_in, sent = refs[:3]
    halves = (refs[3:8], refs[8:13])
    gram, cross, lhs, sides, right = refs[13:]
    block = right.shape[1]
    width = block // 2
    rows = lhs.shape[0] // 2
    step = rows // 2
    here = where[1] == 1
    for h, (a, b, there, raw, scale) in enumerate(halves):
        place = pl.multiple_of((where[0] if h == 0 else 1 - where[0]) * block, block)
        for c, x in enumerate((a, b)):
            window = slice(h * rows + c * step, h * rows + (c + 1) * step)
            lhs[window, :] = x[:, h * block : (h + 1) * block]
            right[window, :] = jnp.where(here, x[:, pl.ds(place, block)], there[c * step : (c + 1) * step, :])
        sides[h * rows : (h + 1) * rows, :] = (scale[...] * raw[...].astype(f32)).astype(bf16)
    mine = pl.multiple_of(where[2] * width, width)

    def product(a, b):
        return lax.dot_general(a, b, contract_first, preferred_element_type=f32)

    part = gram_in[...] + sent[:block, :].astype(f32)
    gram[...] = (part + product(lhs[...], right[...])) * (1.0 / count)
    tall = cross.shape[0] // 2
    part = product(sides[...], right[:, pl.ds(mine, width)])
    for i in range(2):
        window = slice(i * tall, (i + 1) * tall)
        total = part[window] + cross_in[window, :] + sent[block:, i * width : (i + 1) * width].astype(f32)
        cross[window, :] = total * (1.0 / count)


def group_near(level, half, block):
    atoms = 2 * block
    parts = [lax.dynamic_slice_in_dim(level, i * atoms + half * block, block, 1) for i in range(2)]
    return jnp.concatenate(parts, 1)


def paired(patches, dictionary, threshold):
    n_patch = lax.axis_size("patch")
    plane = lax.axis_index("patch")
    core = lax.axis_index("atom")
    half = lax.axis_index("feat")
    count = patches.shape[0] * n_patch
    length = patches.shape[1]
    rows = patches.shape[0] // 2
    atoms = dictionary.shape[1]
    block = atoms // 2
    width = block // 2
    step = rows // 2

    def blocks(array, which):
        return lax.dynamic_slice_in_dim(array, which * block, block, 1)

    mine = lax.dynamic_slice_in_dim(patches, core * rows, rows, 0)
    dictionary2 = swap(dictionary, "atom")
    raw_of = [mine]
    for k in range(1, n_patch):
        raw_of.append(shift(raw_of[-1]))
    windows = [slice(c * step, (c + 1) * step) for c in range(2)]
    parts, others = [], []
    done = ()
    for w in windows:
        piece = after(mine[w], done)
        part = run(
            first_body, jax.ShapeDtypeStruct((step, 2 * atoms), bf16), (half,), (piece, dictionary, dictionary2)
        )
        parts.append(part)
        others.append(swap(part, "feat"))
        done = part
    values = after(mine, parts[0]).astype(f32)
    local_sq = jnp.sum(values * values, axis=1)
    energy = local_sq + swap(local_sq, "feat")
    scale = lax.rsqrt(energy / (BINS * VOXELS) + 1e-05)
    scale_of = [scale[:, None]]
    for k in range(1, n_patch):
        scale_of.append(shift(scale_of[-1][:, 0])[:, None])
    level = threshold[None, :]
    level = jnp.concatenate([level, swap(after(level, parts[1]), "atom")], 1)

    base, backs = [], []
    for c, w in enumerate(windows):
        away, so_far = run(
            second_body,
            (jax.ShapeDtypeStruct((step, atoms), bf16), jax.ShapeDtypeStruct((step, atoms), f32)),
            (half,),
            (parts[c], after(others[c], raw_of[c + 1]), mine[w], scale_of[0][w], level, dictionary, dictionary2),
            [pltpu.VMEM((step, 2 * atoms), bf16)],
        )
        backs.append(swap(away, "feat"))
        base.append(so_far)

    codes_of = []
    done = ()
    for c in range(2):
        back = after(backs[c], done).astype(f32)
        codes_of.append(soft(base[c] + step_rate * back, step_rate * group_near(level, half, block)).astype(bf16))
        done = (codes_of[c], raw_of[-1])

    rings = [codes_of]
    for k in range(1, n_patch):
        rings.append([shift(x) for x in rings[-1]])
    inside = jnp.concatenate(codes_of, 0)
    outside = swap(inside, "feat")

    home_half = plane % 2
    place = jnp.where(core == plane // 2, 0, 1)
    over = [(q * 2 + q % 2, q * 2 + 1 - q % 2) for q in range(n_patch)]
    below = (plane + n_patch - 1) % n_patch
    place_below = jnp.where(core == below // 2, 0, 1)
    down = [
        (q * 2 + 1 - (q - 1) % n_patch % 2, (q - 1) % n_patch * 2 + 1 - (q - 1) % n_patch % 2) for q in range(n_patch)
    ]
    there = [outside]
    for k in range(1, n_patch - 1):
        there.append(
            lax.ppermute(jnp.concatenate([blocks(x, place) for x in rings[k]], 0), ("patch", "feat"), over)
        )
    final = lax.ppermute(blocks(outside, place_below), ("patch", "feat"), down)
    final2 = swap(final, "atom")

    both = [jnp.where(half == 0, inside, outside), jnp.where(half == 0, outside, inside)]
    upper = jnp.concatenate([x[:, :block] for x in both], 1)
    lower = swap(jnp.concatenate([x[:, block:] for x in both], 1), "atom")
    lower = after(lower, rings[1])
    codes = jnp.where(
        core == 0, jnp.concatenate([upper, lower], 0), jnp.concatenate([lower, upper], 0)
    )

    n = n_patch - 1
    at_home = half == home_half
    zero = jnp.zeros_like(place)
    pieces = []
    for k in range(n):
        pieces += [*rings[k], there[k], raw_of[k], scale_of[k]]
    gram, cross, send = run(
        functools.partial(sums_body, n),
        (
            jax.ShapeDtypeStruct((block, block), f32),
            jax.ShapeDtypeStruct((length, width), f32),
            jax.ShapeDtypeStruct((block + length // 2, block), bf16),
        ),
        (place, at_home, core, place) + (zero,) * (n - 1),
        pieces,
        [pltpu.VMEM((n * rows, size), bf16) for size in (atoms, length, block)],
    )
    sent = swap(send, "atom")
    raw2, scale2 = swap(after(raw_of[-1], rings[1]), "atom"), swap(after(scale_of[-1][:, 0], rings[1]), "atom")
    early, late = [swap(x, "atom") for x in rings[-1]]
    early, codes = lax.optimization_barrier((early, codes))
    gram, cross = run(
        functools.partial(last_body, count),
        (jax.ShapeDtypeStruct((block, block), f32), jax.ShapeDtypeStruct((length, width), f32)),
        (place, at_home, core),
        (gram, cross, sent, *rings[-1], final, raw_of[-1], scale_of[-1], early, late, final2, raw2, scale2[:, None]),
        [pltpu.VMEM((2 * rows, size), bf16) for size in (block, length, block)],
    )
    return (codes, gram, cross)


def solution(mesh):
    in_specs = (P(("slab", "patch"), "feat"), P("feat", "atom"), P("atom"))
    out_specs = (
        P(("slab", "patch"), "atom"),
        P(("slab", "atom", "feat"), "patch"),
        P(("slab", "feat"), ("patch", "atom")),
    )
    sizes = mesh.shape
    small = sizes["feat"] == 2 and sizes["atom"] == 2 and sizes["patch"] == 4
    return jax.shard_map(
        paired if small else general, mesh=mesh, in_specs=in_specs, out_specs=out_specs, check_vma=False
    )
```

```python
import functools

import jax
import jax.numpy as jnp
from jax import lax
from jax.experimental import pallas as pl
from jax.experimental.pallas import tpu as pltpu
from jax.sharding import PartitionSpec as P

BINS = 8
VOXELS = 216


step_rate = 0.2


def soften(value, level):
    return jnp.sign(value) * jnp.maximum(jnp.abs(value) - level, 0.0)


def general(patches, dictionary, threshold):
    values = patches.astype(jnp.float32)
    local_sq = jnp.sum(values * values, axis=1)
    local_first = jnp.dot(patches, dictionary, preferred_element_type=jnp.float32)
    summed, energy = lax.psum((local_first, local_sq), "feat")
    scale = lax.rsqrt(energy[:, None] / (BINS * VOXELS) + 1e-05)
    level = step_rate * threshold[None, :]
    start = soften(step_rate * (scale * summed), level).astype(jnp.bfloat16)
    contract_last = (((1,), (1,)), ((), ()))
    own_part = lax.dot_general(start, dictionary, contract_last, preferred_element_type=jnp.float32)
    rebuilt = lax.psum(own_part, "atom")
    misfit = (scale * values - rebuilt).astype(jnp.bfloat16)
    local_second = jnp.dot(misfit, dictionary, preferred_element_type=jnp.float32)
    second = lax.psum(local_second, "feat")
    codes = soften(start.astype(jnp.float32) + step_rate * second, level).astype(jnp.bfloat16)
    codes_whole = lax.all_gather(codes, "atom", axis=1, tiled=True)
    n_patch = lax.axis_size("patch")
    n_atom = lax.axis_size("atom")
    n_feat = lax.axis_size("feat")
    total_atoms = codes_whole.shape[1]
    count = patches.shape[0] * n_patch
    contract_first = (((0,), (0,)), ((), ()))
    block_rows = total_atoms // (n_atom * n_feat)
    offset = (lax.axis_index("atom") * n_feat + lax.axis_index("feat")) * block_rows
    chosen = lax.dynamic_slice_in_dim(codes_whole, offset, block_rows, 1)
    gram_part = lax.dot_general(
        chosen, codes_whole, contract_first, preferred_element_type=jnp.float32
    )
    gram = (
        lax.psum_scatter(
            gram_part.astype(jnp.bfloat16), "patch", scatter_dimension=1, tiled=True
        ).astype(jnp.float32)
        / count
    )
    width = total_atoms // (n_patch * n_atom)
    arranged = codes_whole.reshape(codes_whole.shape[0], n_patch, n_atom, width)
    picked = lax.dynamic_slice_in_dim(arranged, lax.axis_index("atom"), 1, 2).reshape(
        codes_whole.shape[0], n_patch * width
    )
    normed = (scale * values).astype(jnp.bfloat16)
    cross_part = lax.dot_general(normed, picked, contract_first, preferred_element_type=jnp.float32)
    cross = (
        lax.psum_scatter(
            cross_part.astype(jnp.bfloat16), "patch", scatter_dimension=1, tiled=True
        ).astype(jnp.float32)
        / count
    )
    return (codes, gram, cross)


def swap(value, axis):
    return lax.ppermute(value, axis, [(0, 1), (1, 0)])


def shift(value, by=1):
    n = lax.axis_size("patch")
    return lax.ppermute(value, "patch", [(i, (i + by) % n) for i in range(n)])


def after(value, earlier):
    return lax.optimization_barrier((value, earlier))[0]


f32, bf16 = jnp.float32, jnp.bfloat16
contract_last = (((1,), (1,)), ((), ()))
contract_first = (((0,), (0,)), ((), ()))


def soft(value, level):
    return jnp.where(value > level, value - level, jnp.where(value < -level, value + level, 0.0))


def run(body, outs, scalars, arrays, scratch=()):
    fast = pl.BlockSpec(memory_space=pltpu.VMEM)
    slow = pl.BlockSpec(memory_space=pltpu.SMEM)
    return pl.pallas_call(
        body,
        out_shape=outs,
        in_specs=[slow] + [fast] * len(arrays),
        out_specs=jax.tree.map(lambda _: fast, outs),
        scratch_shapes=scratch,
        compiler_params=pltpu.CompilerParams(vmem_limit_bytes=24 << 20),
        cost_estimate=pl.CostEstimate(flops=1000, bytes_accessed=1000, transcendentals=0),
    )(jnp.stack([x.astype(jnp.int32) for x in scalars]), *arrays)


def column(row):
    n = row.shape[1]
    same = lax.broadcasted_iota(jnp.int32, (n, n), 0) == lax.broadcasted_iota(jnp.int32, (n, n), 1)
    return jnp.sum(jnp.where(same, row, 0.0), axis=1, keepdims=True)


def first_body(_, mine, d, out):
    out[...] = jnp.dot(mine[...], d[...], preferred_element_type=f32).astype(bf16)


def copy_body(_, array, out):
    out[...] = array[...]


def second_body(where, part, arrived, part2, arrived2, mine, scale, threshold, own, other, away_a, away_b, misfit, start):
    atoms = own.shape[1]
    block = atoms // 2
    step = away_a.shape[0]
    far = pl.multiple_of((1 - where[0]) * block, block)
    factor = column(scale[...])
    for i, (x, y) in enumerate(((part, arrived), (part2, arrived2))):
        columns = slice(i * atoms, (i + 1) * atoms)
        summed = x[...].astype(f32) + y[...].astype(f32)
        start[:, columns] = soft(step_rate * (factor * summed), step_rate * threshold[:, columns]).astype(bf16)
    rebuilt = sum(
        lax.dot_general(start[:, i * atoms : (i + 1) * atoms], d[...], contract_last, preferred_element_type=f32)
        for i, d in enumerate((own, other))
    )
    misfit[...] = (factor * mine[...].astype(f32) - rebuilt).astype(bf16)
    for i, d in enumerate((own, other)):
        columns = slice(i * block, (i + 1) * block)
        second = jnp.dot(misfit[...], d[:, pl.ds(far, block)], preferred_element_type=f32).astype(bf16)
        away_a[:, columns] = second[:step]
        away_b[:, columns] = second[step:]


def base_body(where, misfit, start, own, other, base):
    atoms = own.shape[1]
    block = atoms // 2
    near = pl.multiple_of(where[0] * block, block)
    for i, d in enumerate((own, other)):
        second = jnp.dot(misfit[...], d[:, pl.ds(near, block)], preferred_element_type=f32)
        known = start[:, pl.ds(pl.multiple_of(i * atoms + near, block), block)].astype(f32)
        base[:, i * block : (i + 1) * block] = known + step_rate * second


def sums_body(offsets, where, *refs):
    n = len(offsets)
    pieces, totals, (gram, cross, send, lhs, sides, right) = refs[: 6 * n], refs[6 * n : -6], refs[-6:]
    block = right.shape[1]
    width = block // 2
    place = pl.multiple_of(where[0] * block, block)
    here = where[1] == 1
    rows = lhs.shape[0] // n
    step = rows // 2
    for k in range(n):
        for c in range(2):
            x, there, offset = pieces[6 * k + c], pieces[6 * k + 2 + c], offsets[k][c]
            window = slice(k * rows + c * step, k * rows + (c + 1) * step)
            lhs[window, :] = x[...]
            spot = pl.multiple_of(where[3 + k] * block, block)
            right[window, :] = jnp.where(
                here, x[:, pl.ds(place, block)], there[offset : offset + step, pl.ds(spot, block)]
            )
        raw, scale = pieces[6 * k + 4 : 6 * k + 6]
        sides[k * rows : (k + 1) * rows, :] = (column(scale[...]) * raw[...].astype(f32)).astype(bf16)
    mine = pl.multiple_of(where[2] * width, width)
    theirs = pl.multiple_of((1 - where[2]) * width, width)
    tall = sides.shape[1] // 2

    def product(a, b):
        return lax.dot_general(a, b, contract_first, preferred_element_type=f32)

    def store(ref, index, value):
        if totals:
            value += totals[index[0]][index[1]]
        ref[index[1]] = value.astype(ref.dtype)

    part = product(lhs[:, block:], right[...])
    store(send, (2, (slice(0, block), slice(None))), part)
    part = product(sides[...], right[:, pl.ds(theirs, width)])
    store(send, (2, (slice(block, block + tall), slice(0, width))), part[:tall])
    store(send, (2, (slice(block, block + tall), slice(width, block))), part[tall:])
    store(gram, (0, (slice(None), slice(None))), product(lhs[:, :block], right[...]))
    store(cross, (1, (slice(None), slice(None))), product(sides[...], right[:, pl.ds(mine, width)]))


def add_body(count, _, gram_in, cross_in, sent, gram, cross):
    block = gram.shape[0]
    width = cross.shape[1]
    tall = cross.shape[0] // 2
    gram[...] = (gram_in[...] + sent[:block, :].astype(f32)) * (1.0 / count)
    for i in range(2):
        window = slice(i * tall, (i + 1) * tall)
        total = cross_in[window, :] + sent[block:, i * width : (i + 1) * width].astype(f32)
        cross[window, :] = total * (1.0 / count)


def group_near(level, half, block):
    atoms = 2 * block
    parts = [lax.dynamic_slice_in_dim(level, i * atoms + half * block, block, 1) for i in range(2)]
    return jnp.concatenate(parts, 1)


def paired(patches, dictionary, threshold):
    n_patch = lax.axis_size("patch")
    plane = lax.axis_index("patch")
    core = lax.axis_index("atom")
    half = lax.axis_index("feat")
    count = patches.shape[0] * n_patch
    length = patches.shape[1]
    rows = patches.shape[0] // 2
    atoms = dictionary.shape[1]
    block = atoms // 2
    width = block // 2
    step = rows // 2

    def blocks(array, which):
        return lax.dynamic_slice_in_dim(array, which * block, block, 1)

    mine = lax.dynamic_slice_in_dim(patches, core * rows, rows, 0)
    dictionary2 = swap(dictionary, "atom")
    level = threshold[None, :]
    level = jnp.concatenate([level, swap(level, "atom")], 1)
    windows = [slice(c * step, (c + 1) * step) for c in range(2)]

    def project(value, d):
        shape = jax.ShapeDtypeStruct((value.shape[0], d.shape[1]), bf16)
        return run(first_body, shape, (half,), (value, d))

    raw_of = [mine, shift(mine)]
    part = project(mine, dictionary)
    other = swap(part, "feat")
    local_sq = jnp.sum(jnp.square(after(mine, part).astype(f32)), axis=1)
    other_sq = swap(local_sq, "feat")
    part2 = project(after(mine, part), dictionary2)
    other2 = swap(part2, "feat")
    energy = local_sq + after(other_sq, part2)
    scale = lax.rsqrt(energy / (BINS * VOXELS) + 1e-05)
    raw_of.append(shift(after(raw_of[1], part2)))
    held = run(copy_body, jax.ShapeDtypeStruct(dictionary.shape, bf16), (half,), (after(dictionary2, part2),))
    half_shape = jax.ShapeDtypeStruct((step, atoms), bf16)
    away_a, away_b, misfit, start = run(
        second_body,
        (
            half_shape,
            half_shape,
            jax.ShapeDtypeStruct((rows, length), bf16),
            jax.ShapeDtypeStruct((rows, 2 * atoms), bf16),
        ),
        (half,),
        (part, other, part2, other2, mine, scale[None, :], level, dictionary, after(held, raw_of[2])),
    )
    base = run(
        base_body, jax.ShapeDtypeStruct((rows, atoms), f32), (half,), (misfit, start, dictionary, held)
    )
    raw_of.append(shift(raw_of[2]))
    backs = [swap(x, "feat") for x in (away_a, away_b)]
    own_scale = after(scale, away_b)
    scale_of = [scale] + [shift(own_scale, k) for k in range(1, n_patch)]

    near_level = step_rate * group_near(level, half, block)
    codes_of = []
    done = ()
    for c in range(2):
        back = after(backs[c], done).astype(f32)
        codes_of.append(soft(base[windows[c]] + step_rate * back, near_level).astype(bf16))
        done = codes_of[c]

    inside = jnp.concatenate(codes_of, 0)
    ring1 = [shift(x) for x in codes_of]
    ring1 = [after(x, y) for x, y in zip(ring1, (raw_of[3], scale_of))]
    outside = swap(after(inside, ring1[0]), "feat")
    ring2 = [shift(x) for x in ring1]

    home_half = plane % 2
    place = jnp.where(core == plane // 2, 0, 1)
    over = [(q * 2 + q % 2, q * 2 + 1 - q % 2) for q in range(n_patch)]

    def across(arrays):
        return lax.ppermute(jnp.concatenate([blocks(x, place) for x in arrays], 0), ("patch", "feat"), over)

    there1 = across([*ring1, ring2[0]])
    ring2[1] = after(ring2[1], outside)
    ring3 = [shift(x) for x in ring2]
    ring3[0] = after(ring3[0], there1)
    there2 = across([ring2[1], ring3[0]])

    both = [jnp.where(half == 0, inside, outside), jnp.where(half == 0, outside, inside)]
    upper = jnp.concatenate([x[:, :block] for x in both], 1)
    lower = after(jnp.concatenate([x[:, block:] for x in both], 1), ring2[0])
    lower = swap(lower, "atom")
    ring3[0] = after(ring3[0], lower)

    zero = jnp.zeros_like(place)
    rings = (codes_of, ring1, ring2, ring3)
    totals = ()
    for planes, kind in (((0, 1), f32), ((2, 3), bf16)):
        if kind == f32:
            there = ((outside, outside), (there1, there1))
            offsets = ((0, step), (0, step))
        else:
            ring3[1] = after(ring3[1], totals)
            there = ((there1, there2), (there2, across([ring3[1]])))
            offsets = ((2 * step, 0), (step, 0))
        pieces = []
        for i, k in enumerate(planes):
            pieces += [*rings[k], *there[i], raw_of[k], scale_of[k][None, :]]
        totals = run(
            functools.partial(sums_body, offsets),
            (
                jax.ShapeDtypeStruct((block, block), f32),
                jax.ShapeDtypeStruct((length, width), f32),
                jax.ShapeDtypeStruct((block + length // 2, block), kind),
            ),
            (place, half == home_half, core) + tuple(zero if k else place for k in planes),
            (*pieces, *totals),
            [pltpu.VMEM((len(planes) * rows, size), bf16) for size in (atoms, length, block)],
        )
    gram, cross, send = totals
    lower = after(lower, send)
    codes = jnp.where(
        core == 0, jnp.concatenate([upper, lower], 0), jnp.concatenate([lower, upper], 0)
    )
    gram, cross = run(
        functools.partial(add_body, count),
        (jax.ShapeDtypeStruct((block, block), f32), jax.ShapeDtypeStruct((length, width), f32)),
        (half,),
        (gram, cross, after(swap(send, "atom"), codes)),
    )
    return (codes, gram, cross)


def solution(mesh):
    in_specs = (P(("slab", "patch"), "feat"), P("feat", "atom"), P("atom"))
    out_specs = (
        P(("slab", "patch"), "atom"),
        P(("slab", "atom", "feat"), "patch"),
        P(("slab", "feat"), ("patch", "atom")),
    )
    sizes = mesh.shape
    small = sizes["feat"] == 2 and sizes["atom"] == 2 and sizes["patch"] == 4
    return jax.shard_map(
        paired if small else general, mesh=mesh, in_specs=in_specs, out_specs=out_specs, check_vma=False
    )
```

```python
import functools

import jax
import jax.numpy as jnp
from jax import lax
from jax.experimental import pallas as pl
from jax.experimental.pallas import tpu as pltpu
from jax.sharding import PartitionSpec as P

BINS = 8
VOXELS = 216


step_rate = 0.2
ORDER = {
    "square": ("part",),
    "n1 out": ("part",),
    "part2": ("part",),
    "e in": ("part2",),
    "n2 out": ("part2",),
    "held in": ("part2",),
    "second": ("n1 in",),
    "sb out": ("n2 in",),
    "z1a in": ("n3 in",),
    "x out": ("codes b",),
    "e2 out": ("z1a in",),
    "z2b in": ("x in", "e2 in",),
    "c out": ("x in",),
    "qd in": ("codes",),
    "z3b in": ("sums1",),
    "z3a in": ("qb in",),
    "qb out": ("z2b in",),
    "sb in": ("z1a out",),
}


def soften(value, level):
    return jnp.sign(value) * jnp.maximum(jnp.abs(value) - level, 0.0)


def general(patches, dictionary, threshold):
    values = patches.astype(jnp.float32)
    local_sq = jnp.sum(values * values, axis=1)
    local_first = jnp.dot(patches, dictionary, preferred_element_type=jnp.float32)
    summed, energy = lax.psum((local_first, local_sq), "feat")
    scale = lax.rsqrt(energy[:, None] / (BINS * VOXELS) + 1e-05)
    level = step_rate * threshold[None, :]
    start = soften(step_rate * (scale * summed), level).astype(jnp.bfloat16)
    contract_last = (((1,), (1,)), ((), ()))
    own_part = lax.dot_general(start, dictionary, contract_last, preferred_element_type=jnp.float32)
    rebuilt = lax.psum(own_part, "atom")
    misfit = (scale * values - rebuilt).astype(jnp.bfloat16)
    local_second = jnp.dot(misfit, dictionary, preferred_element_type=jnp.float32)
    second = lax.psum(local_second, "feat")
    codes = soften(start.astype(jnp.float32) + step_rate * second, level).astype(jnp.bfloat16)
    codes_whole = lax.all_gather(codes, "atom", axis=1, tiled=True)
    n_patch = lax.axis_size("patch")
    n_atom = lax.axis_size("atom")
    n_feat = lax.axis_size("feat")
    total_atoms = codes_whole.shape[1]
    count = patches.shape[0] * n_patch
    contract_first = (((0,), (0,)), ((), ()))
    block_rows = total_atoms // (n_atom * n_feat)
    offset = (lax.axis_index("atom") * n_feat + lax.axis_index("feat")) * block_rows
    chosen = lax.dynamic_slice_in_dim(codes_whole, offset, block_rows, 1)
    gram_part = lax.dot_general(
        chosen, codes_whole, contract_first, preferred_element_type=jnp.float32
    )
    gram = (
        lax.psum_scatter(
            gram_part.astype(jnp.bfloat16), "patch", scatter_dimension=1, tiled=True
        ).astype(jnp.float32)
        / count
    )
    width = total_atoms // (n_patch * n_atom)
    arranged = codes_whole.reshape(codes_whole.shape[0], n_patch, n_atom, width)
    picked = lax.dynamic_slice_in_dim(arranged, lax.axis_index("atom"), 1, 2).reshape(
        codes_whole.shape[0], n_patch * width
    )
    normed = (scale * values).astype(jnp.bfloat16)
    cross_part = lax.dot_general(normed, picked, contract_first, preferred_element_type=jnp.float32)
    cross = (
        lax.psum_scatter(
            cross_part.astype(jnp.bfloat16), "patch", scatter_dimension=1, tiled=True
        ).astype(jnp.float32)
        / count
    )
    return (codes, gram, cross)


def swap(value, axis):
    return lax.ppermute(value, axis, [(0, 1), (1, 0)])


def shift(value, by=1):
    n = lax.axis_size("patch")
    return lax.ppermute(value, "patch", [(i, (i + by) % n) for i in range(n)])


def after(value, earlier):
    return lax.optimization_barrier((value, earlier))[0]


f32, bf16 = jnp.float32, jnp.bfloat16
contract_last = (((1,), (1,)), ((), ()))
contract_first = (((0,), (0,)), ((), ()))


def soft(value, level):
    return jnp.where(value > level, value - level, jnp.where(value < -level, value + level, 0.0))


def run(body, outs, scalars, arrays, scratch=()):
    fast = pl.BlockSpec(memory_space=pltpu.VMEM)
    slow = pl.BlockSpec(memory_space=pltpu.SMEM)
    return pl.pallas_call(
        body,
        out_shape=outs,
        in_specs=[slow] + [fast] * len(arrays),
        out_specs=jax.tree.map(lambda _: fast, outs),
        scratch_shapes=scratch,
        compiler_params=pltpu.CompilerParams(vmem_limit_bytes=8 << 20),
        cost_estimate=pl.CostEstimate(flops=1000, bytes_accessed=1000, transcendentals=0),
    )(jnp.stack([x.astype(jnp.int32) for x in scalars]), *arrays)


def column(row):
    n = row.shape[1]
    same = lax.broadcasted_iota(jnp.int32, (n, n), 0) == lax.broadcasted_iota(jnp.int32, (n, n), 1)
    return jnp.sum(jnp.where(same, row, 0.0), axis=1, keepdims=True)


def first_body(_, mine, d, out):
    out[...] = jnp.dot(mine[...], d[...], preferred_element_type=f32).astype(bf16)


def copy_body(_, array, out):
    out[...] = array[...]


def second_body(where, part, arrived, part2, arrived2, mine, scale, threshold, own, other, away_a, away_b, misfit, start):
    atoms = own.shape[1]
    block = atoms // 2
    step = away_a.shape[0]
    far = pl.multiple_of((1 - where[0]) * block, block)
    factor = column(scale[...])
    for i, (x, y) in enumerate(((part, arrived), (part2, arrived2))):
        columns = slice(i * atoms, (i + 1) * atoms)
        summed = x[...].astype(f32) + y[...].astype(f32)
        start[:, columns] = soft(step_rate * (factor * summed), step_rate * threshold[:, columns]).astype(bf16)
    rebuilt = sum(
        lax.dot_general(start[:, i * atoms : (i + 1) * atoms], d[...], contract_last, preferred_element_type=f32)
        for i, d in enumerate((own, other))
    )
    misfit[...] = (factor * mine[...].astype(f32) - rebuilt).astype(bf16)
    for i, d in enumerate((own, other)):
        columns = slice(i * block, (i + 1) * block)
        second = jnp.dot(misfit[...], d[:, pl.ds(far, block)], preferred_element_type=f32).astype(bf16)
        away_a[:, columns] = second[:step]
        away_b[:, columns] = second[step:]


def base_body(where, misfit, start, own, other, base):
    atoms = own.shape[1]
    block = atoms // 2
    near = pl.multiple_of(where[0] * block, block)
    for i, d in enumerate((own, other)):
        second = jnp.dot(misfit[...], d[:, pl.ds(near, block)], preferred_element_type=f32)
        known = start[:, pl.ds(pl.multiple_of(i * atoms + near, block), block)].astype(f32)
        base[:, i * block : (i + 1) * block] = known + step_rate * second


def sums_body(segments, sides_of, where, *refs):
    n = len(segments)
    m = len(sides_of)
    pieces, totals = refs[: 4 * n], refs[4 * n : -3 - m]
    outs, (lhs, sides, right) = refs[-3 - m : -3], refs[-3:]
    block = right.shape[1]
    width = block // 2
    place = pl.multiple_of(where[0] * block, block)
    here = where[1] == 1
    step = lhs.shape[0] // n
    for k, (offset, base, entry) in enumerate(segments):
        x, there, raw, scale = pieces[4 * k : 4 * k + 4]
        window = slice(k * step, (k + 1) * step)
        lhs[window, :] = x[...]
        spot = pl.multiple_of(where[entry] * block, block)
        right[window, :] = jnp.where(
            here, x[:, pl.ds(place, block)], there[offset : offset + step, pl.ds(spot, block)]
        )
        factor = column(scale[...])[base : base + step]
        sides[window, :] = (factor * raw[base : base + step, :].astype(f32)).astype(bf16)
    mine = pl.multiple_of(where[2] * width, width)
    theirs = pl.multiple_of((1 - where[2]) * width, width)
    tall = sides.shape[1] // 2

    def product(a, b):
        return lax.dot_general(a, b, contract_first, preferred_element_type=f32)

    for i, ours in enumerate(sides_of):
        left, columns = (slice(0, block), mine) if ours else (slice(block, 2 * block), theirs)
        for window, value in (
            ((slice(0, block), slice(0, block)), product(lhs[:, left], right[...])),
            ((slice(block, block + tall), slice(0, width)), product(sides[:, :tall], right[:, pl.ds(columns, width)])),
            ((slice(block, block + tall), slice(width, block)), product(sides[:, tall:], right[:, pl.ds(columns, width)])),
        ):
            if totals:
                value += totals[i][window]
            outs[i][window] = value.astype(outs[i].dtype)


def add_body(count, _, kept, sent, gram, cross):
    block = gram.shape[0]
    width = cross.shape[1]
    tall = cross.shape[0] // 2
    gram[...] = (kept[:block, :] + sent[:block, :].astype(f32)) * (1.0 / count)
    for i in range(2):
        window = slice(i * width, (i + 1) * width)
        total = kept[block:, window] + sent[block:, window].astype(f32)
        cross[i * tall : (i + 1) * tall, :] = total * (1.0 / count)


def group_near(level, half, block):
    atoms = 2 * block
    parts = [lax.dynamic_slice_in_dim(level, i * atoms + half * block, block, 1) for i in range(2)]
    return jnp.concatenate(parts, 1)


def paired(patches, dictionary, threshold):
    n_patch = lax.axis_size("patch")
    plane = lax.axis_index("patch")
    core = lax.axis_index("atom")
    half = lax.axis_index("feat")
    count = patches.shape[0] * n_patch
    length = patches.shape[1]
    rows = patches.shape[0] // 2
    atoms = dictionary.shape[1]
    block = atoms // 2
    width = block // 2
    step = rows // 2
    there_is = {}

    def tie(name, value):
        earlier = [there_is[x] for x in ORDER.get(name, ())]
        there_is[name] = after(value, earlier) if earlier else value
        return there_is[name]

    def send(name, value, how):
        return how(tie(name + " out", value))

    def over_feat(value):
        return swap(value, "feat")

    def over_cores(value):
        return swap(value, "atom")

    def blocks(array, which):
        return lax.dynamic_slice_in_dim(array, which * block, block, 1)

    def project(value, d):
        shape = jax.ShapeDtypeStruct((value.shape[0], d.shape[1]), bf16)
        return run(first_body, shape, (half,), (value, d))

    def scale_from(energy):
        return lax.rsqrt(energy / (BINS * VOXELS) + 1e-05)

    mine = lax.dynamic_slice_in_dim(patches, core * rows, rows, 0)
    dictionary2 = tie("d in", send("d", dictionary, over_cores))
    level = threshold[None, :]
    level2 = send("level", level, over_cores)
    part = project(tie("part", mine), dictionary)
    there_is["part"] = part
    other = send("f1", part, over_feat)
    raw_of = [mine, send("n1", mine, shift)]
    local_sq = jnp.sum(jnp.square(tie("square", mine).astype(f32)), axis=1)
    other_sq = send("e", local_sq, over_feat)
    part2 = project(tie("part2", mine), dictionary2)
    there_is["part2"] = part2
    other2 = send("f2", part2, over_feat)
    raw_of[1] = tie("n1 in", raw_of[1])
    raw_of.append(send("n2", raw_of[1], shift))
    level = jnp.concatenate([level, tie("level in", level2)], 1)
    scale = scale_from(local_sq + tie("e in", other_sq))
    held = tie("held in", dictionary2)
    held = run(copy_body, jax.ShapeDtypeStruct(dictionary.shape, bf16), (half,), (held,))
    there_is["held"] = held
    other, other2 = tie("f1 in", other), tie("f2 in", other2)

    half_shape = jax.ShapeDtypeStruct((step, atoms), bf16)
    away_a, away_b, misfit, start = run(
        second_body,
        (
            half_shape,
            half_shape,
            jax.ShapeDtypeStruct((rows, length), bf16),
            jax.ShapeDtypeStruct((rows, 2 * atoms), bf16),
        ),
        (half,),
        (part, other, part2, other2, mine, scale[None, :], level, dictionary, tie("second", held)),
    )
    there_is["second"] = away_a
    raw_of[2] = tie("n2 in", raw_of[2])
    raw_of.append(send("n3", raw_of[2], shift))
    back_a = send("sa", away_a, over_feat)
    back_b = send("sb", away_b, over_feat)
    base = run(
        base_body, jax.ShapeDtypeStruct((rows, atoms), f32), (half,), (tie("base", misfit), start, dictionary, held)
    )
    there_is["base"] = base

    near_level = step_rate * group_near(level, half, block)

    def codes_from(back, window):
        return soft(base[window] + step_rate * back.astype(f32), near_level).astype(bf16)

    codes_of = [codes_from(tie("sa in", back_a), slice(0, step))]
    there_is["codes a"] = codes_of[0]
    ring1 = [send("z1a", codes_of[0], shift)]
    codes_of.append(codes_from(tie("sb in", back_b), slice(step, rows)))
    there_is["codes b"] = codes_of[1]
    ring1.append(send("z1b", codes_of[1], shift))
    raw_of[3] = tie("n3 in", raw_of[3])
    ring1[0] = tie("z1a in", ring1[0])
    ring2 = [send("z2a", ring1[0], shift)]
    inside = jnp.concatenate(codes_of, 0)
    outside = send("x", inside, over_feat)
    sums = jnp.concatenate([jnp.sum(jnp.square(x.astype(f32)), axis=1) for x in raw_of[1:]])
    sums += tie("e2 in", send("e2", sums, over_feat))
    scales = scale_from(sums)
    scale_of = [scale] + [scales[k * rows : (k + 1) * rows] for k in range(n_patch - 1)]

    home_half = plane % 2
    place = jnp.where(core == plane // 2, 0, 1)
    def own_block(arrays):
        return jnp.concatenate([blocks(x, place) for x in arrays], 0)

    outside = tie("x in", outside)
    ring1[1] = tie("z1b in", ring1[1])
    ring2.append(send("z2b", ring1[1], shift))
    def whole_codes():
        both = [jnp.where(half == 0, inside, outside), jnp.where(half == 0, outside, inside)]
        upper = jnp.concatenate([x[:, :block] for x in both], 1)
        lower = send("c", jnp.concatenate([x[:, block:] for x in both], 1), over_cores)
        lower = tie("c in", lower)
        there_is["codes"] = jnp.where(
            core == 0, jnp.concatenate([upper, lower], 0), jnp.concatenate([lower, upper], 0)
        )
        return there_is["codes"]

    ring2[0] = tie("z2a in", ring2[0])
    ring3 = [send("z3a", ring2[0], shift)]
    codes = whole_codes()
    ring2[1] = tie("z2b in", ring2[1])
    ring3.append(send("z3b", ring2[1], shift))
    there1 = send("qa", own_block(ring1), over_feat)
    there2 = send("qb", own_block(ring2), over_feat)
    there1 = tie("qa in", there1)
    rings = (codes_of, ring1, ring2, ring3)

    def add_products(name, segments, kinds, totals=()):
        pieces = []
        for i, (k, c, there, _) in enumerate(segments):
            pieces += [rings[k][c], there if i else tie(name, there), raw_of[k], scale_of[k][None, :]]
        totals = run(
            functools.partial(
                sums_body, [(offset, c * step, 4 if k else 3) for k, c, _, offset in segments], tuple(kinds)
            ),
            [jax.ShapeDtypeStruct((block + length // 2, block), x) for x in kinds.values()],
            (place, half == home_half, core, place, jnp.zeros_like(place)),
            (*pieces, *totals),
            [pltpu.VMEM((len(segments) * step, size), bf16) for size in (atoms, length, block)],
        )
        there_is[name] = totals[0]
        return totals

    first = [(0, 0, outside, 0), (0, 1, outside, step), (1, 0, there1, 0), (1, 1, there1, step)]
    totals = add_products("sums1", first, {False: f32, True: f32})
    there2 = tie("qb in", there2)
    ring3[0] = tie("z3a in", ring3[0])
    there3 = [send("qc", own_block(ring3[:1]), over_feat)]
    second = [(2, 0, there2, 0), (2, 1, there2, step)]
    totals = add_products("sums2", second, {False: f32, True: f32}, totals)
    ring3[1] = tie("z3b in", ring3[1])
    there3.append(send("qd", own_block(ring3[1:]), over_feat))
    there3[0] = tie("qc in", there3[0])
    there3[1] = tie("qd in", there3[1])
    third = [(3, 0, there3[0], 0), (3, 1, there3[1], 0)]
    (total,) = add_products("sums3", third, {False: bf16}, totals[:1])
    sent = tie("sent in", send("sent", total, over_cores))
    third = [(3, 0, after(there3[0], total), 0), (3, 1, there3[1], 0)]
    (kept,) = add_products("sums4", third, {True: f32}, totals[1:])
    gram, cross = run(
        functools.partial(add_body, count),
        (jax.ShapeDtypeStruct((block, block), f32), jax.ShapeDtypeStruct((length, width), f32)),
        (half,),
        (kept, sent),
    )
    return (codes, gram, cross)


def solution(mesh):
    in_specs = (P(("slab", "patch"), "feat"), P("feat", "atom"), P("atom"))
    out_specs = (
        P(("slab", "patch"), "atom"),
        P(("slab", "atom", "feat"), "patch"),
        P(("slab", "feat"), ("patch", "atom")),
    )
    sizes = mesh.shape
    small = sizes["feat"] == 2 and sizes["atom"] == 2 and sizes["patch"] == 4
    return jax.shard_map(
        paired if small else general, mesh=mesh, in_specs=in_specs, out_specs=out_specs, check_vma=False
    )
```

```python
import functools

import jax
import jax.numpy as jnp
from jax import lax
from jax.experimental import pallas as pl
from jax.experimental.pallas import tpu as pltpu
from jax.sharding import PartitionSpec as P

BINS = 8
VOXELS = 216


step_rate = 0.2
ORDER = {
    "square": ("part",),
    "n1 out": ("part",),
    "part2": ("part",),
    "e in": ("part2",),
    "n2 out": ("part2",),
    "held in": ("part2",),
    "second": ("n1 in",),
    "sb out": ("n2 in",),
    "z1a in": ("n3 in",),
    "e2 out": ("z1a in",),
    "z2b in": ("x in", "e2 in",),
    "c out": ("z1b in",),
    "z3b in": ("sums1",),
    "z3a in": ("qa in",),
    "sb in": ("z1a out",),
    "z1b in": ("e2 in",),
    "sums2": ("codes",),
}


def soften(value, level):
    return jnp.sign(value) * jnp.maximum(jnp.abs(value) - level, 0.0)


def general(patches, dictionary, threshold):
    values = patches.astype(jnp.float32)
    local_sq = jnp.sum(values * values, axis=1)
    local_first = jnp.dot(patches, dictionary, preferred_element_type=jnp.float32)
    summed, energy = lax.psum((local_first, local_sq), "feat")
    scale = lax.rsqrt(energy[:, None] / (BINS * VOXELS) + 1e-05)
    level = step_rate * threshold[None, :]
    start = soften(step_rate * (scale * summed), level).astype(jnp.bfloat16)
    contract_last = (((1,), (1,)), ((), ()))
    own_part = lax.dot_general(start, dictionary, contract_last, preferred_element_type=jnp.float32)
    rebuilt = lax.psum(own_part, "atom")
    misfit = (scale * values - rebuilt).astype(jnp.bfloat16)
    local_second = jnp.dot(misfit, dictionary, preferred_element_type=jnp.float32)
    second = lax.psum(local_second, "feat")
    codes = soften(start.astype(jnp.float32) + step_rate * second, level).astype(jnp.bfloat16)
    codes_whole = lax.all_gather(codes, "atom", axis=1, tiled=True)
    n_patch = lax.axis_size("patch")
    n_atom = lax.axis_size("atom")
    n_feat = lax.axis_size("feat")
    total_atoms = codes_whole.shape[1]
    count = patches.shape[0] * n_patch
    contract_first = (((0,), (0,)), ((), ()))
    block_rows = total_atoms // (n_atom * n_feat)
    offset = (lax.axis_index("atom") * n_feat + lax.axis_index("feat")) * block_rows
    chosen = lax.dynamic_slice_in_dim(codes_whole, offset, block_rows, 1)
    gram_part = lax.dot_general(
        chosen, codes_whole, contract_first, preferred_element_type=jnp.float32
    )
    gram = (
        lax.psum_scatter(
            gram_part.astype(jnp.bfloat16), "patch", scatter_dimension=1, tiled=True
        ).astype(jnp.float32)
        / count
    )
    width = total_atoms // (n_patch * n_atom)
    arranged = codes_whole.reshape(codes_whole.shape[0], n_patch, n_atom, width)
    picked = lax.dynamic_slice_in_dim(arranged, lax.axis_index("atom"), 1, 2).reshape(
        codes_whole.shape[0], n_patch * width
    )
    normed = (scale * values).astype(jnp.bfloat16)
    cross_part = lax.dot_general(normed, picked, contract_first, preferred_element_type=jnp.float32)
    cross = (
        lax.psum_scatter(
            cross_part.astype(jnp.bfloat16), "patch", scatter_dimension=1, tiled=True
        ).astype(jnp.float32)
        / count
    )
    return (codes, gram, cross)


def swap(value, axis):
    return lax.ppermute(value, axis, [(0, 1), (1, 0)])


def shift(value, by=1):
    n = lax.axis_size("patch")
    return lax.ppermute(value, "patch", [(i, (i + by) % n) for i in range(n)])


def after(value, earlier):
    return lax.optimization_barrier((value, earlier))[0]


f32, bf16 = jnp.float32, jnp.bfloat16
contract_last = (((1,), (1,)), ((), ()))
contract_first = (((0,), (0,)), ((), ()))


def soft(value, level):
    return jnp.where(value > level, value - level, jnp.where(value < -level, value + level, 0.0))


def run(body, outs, scalars, arrays, scratch=()):
    fast = pl.BlockSpec(memory_space=pltpu.VMEM)
    slow = pl.BlockSpec(memory_space=pltpu.SMEM)
    return pl.pallas_call(
        body,
        out_shape=outs,
        in_specs=[slow] + [fast] * len(arrays),
        out_specs=jax.tree.map(lambda _: fast, outs),
        scratch_shapes=scratch,
        compiler_params=pltpu.CompilerParams(vmem_limit_bytes=8 << 20),
        cost_estimate=pl.CostEstimate(flops=1000, bytes_accessed=1000, transcendentals=0),
    )(jnp.stack([x.astype(jnp.int32) for x in scalars]), *arrays)


def column(row):
    n = row.shape[1]
    same = lax.broadcasted_iota(jnp.int32, (n, n), 0) == lax.broadcasted_iota(jnp.int32, (n, n), 1)
    return jnp.sum(jnp.where(same, row, 0.0), axis=1, keepdims=True)


def first_body(_, mine, d, out):
    out[...] = jnp.dot(mine[...], d[...], preferred_element_type=f32).astype(bf16)


def copy_body(_, array, out):
    out[...] = array[...]


def second_body(where, part, arrived, part2, arrived2, mine, scale, threshold, own, other, away_a, away_b, misfit, start):
    atoms = own.shape[1]
    block = atoms // 2
    step = away_a.shape[0]
    far = pl.multiple_of((1 - where[0]) * block, block)
    factor = column(scale[...])
    for i, (x, y) in enumerate(((part, arrived), (part2, arrived2))):
        columns = slice(i * atoms, (i + 1) * atoms)
        summed = x[...].astype(f32) + y[...].astype(f32)
        start[:, columns] = soft(step_rate * (factor * summed), step_rate * threshold[:, columns]).astype(bf16)
    rebuilt = sum(
        lax.dot_general(start[:, i * atoms : (i + 1) * atoms], d[...], contract_last, preferred_element_type=f32)
        for i, d in enumerate((own, other))
    )
    misfit[...] = (factor * mine[...].astype(f32) - rebuilt).astype(bf16)
    for i, d in enumerate((own, other)):
        columns = slice(i * block, (i + 1) * block)
        second = jnp.dot(misfit[...], d[:, pl.ds(far, block)], preferred_element_type=f32).astype(bf16)
        away_a[:, columns] = second[:step]
        away_b[:, columns] = second[step:]


def base_body(where, misfit, start, own, other, base):
    atoms = own.shape[1]
    block = atoms // 2
    near = pl.multiple_of(where[0] * block, block)
    for i, d in enumerate((own, other)):
        second = jnp.dot(misfit[...], d[:, pl.ds(near, block)], preferred_element_type=f32)
        known = start[:, pl.ds(pl.multiple_of(i * atoms + near, block), block)].astype(f32)
        base[:, i * block : (i + 1) * block] = known + step_rate * second


def sums_body(segments, sides_of, where, *refs):
    n = len(segments)
    m = len(sides_of)
    pieces, totals = refs[: 4 * n], refs[4 * n : -3 - m]
    outs, (lhs, sides, right) = refs[-3 - m : -3], refs[-3:]
    block = right.shape[1]
    width = block // 2
    place = pl.multiple_of(where[0] * block, block)
    here = where[1] == 1
    step = lhs.shape[0] // n
    for k, (offset, base, entry) in enumerate(segments):
        x, there, raw, scale = pieces[4 * k : 4 * k + 4]
        window = slice(k * step, (k + 1) * step)
        lhs[window, :] = x[...]
        spot = pl.multiple_of(where[entry] * block, block)
        right[window, :] = jnp.where(
            here, x[:, pl.ds(place, block)], there[offset : offset + step, pl.ds(spot, block)]
        )
        factor = column(scale[...])[base : base + step]
        sides[window, :] = (factor * raw[base : base + step, :].astype(f32)).astype(bf16)
    mine = pl.multiple_of(where[2] * width, width)
    theirs = pl.multiple_of((1 - where[2]) * width, width)
    tall = sides.shape[1] // 2

    def product(a, b):
        return lax.dot_general(a, b, contract_first, preferred_element_type=f32)

    for i, ours in enumerate(sides_of):
        left, columns = (slice(0, block), mine) if ours else (slice(block, 2 * block), theirs)
        for window, value in (
            ((slice(0, block), slice(0, block)), product(lhs[:, left], right[...])),
            ((slice(block, block + tall), slice(0, width)), product(sides[:, :tall], right[:, pl.ds(columns, width)])),
            ((slice(block, block + tall), slice(width, block)), product(sides[:, tall:], right[:, pl.ds(columns, width)])),
        ):
            if totals:
                value += totals[i][window]
            outs[i][window] = value.astype(outs[i].dtype)


def add_body(count, _, kept, sent, gram, cross):
    block = gram.shape[0]
    width = cross.shape[1]
    tall = cross.shape[0] // 2
    gram[...] = (kept[:block, :] + sent[:block, :].astype(f32)) * (1.0 / count)
    for i in range(2):
        window = slice(i * width, (i + 1) * width)
        total = kept[block:, window] + sent[block:, window].astype(f32)
        cross[i * tall : (i + 1) * tall, :] = total * (1.0 / count)


def group_near(level, half, block):
    atoms = 2 * block
    parts = [lax.dynamic_slice_in_dim(level, i * atoms + half * block, block, 1) for i in range(2)]
    return jnp.concatenate(parts, 1)


def paired(patches, dictionary, threshold):
    n_patch = lax.axis_size("patch")
    plane = lax.axis_index("patch")
    core = lax.axis_index("atom")
    half = lax.axis_index("feat")
    count = patches.shape[0] * n_patch
    length = patches.shape[1]
    rows = patches.shape[0] // 2
    atoms = dictionary.shape[1]
    block = atoms // 2
    width = block // 2
    step = rows // 2
    there_is = {}

    def tie(name, value):
        earlier = [there_is[x] for x in ORDER.get(name, ())]
        there_is[name] = after(value, earlier) if earlier else value
        return there_is[name]

    def send(name, value, how):
        return how(tie(name + " out", value))

    def over_feat(value):
        return swap(value, "feat")

    def over_cores(value):
        return swap(value, "atom")

    def blocks(array, which):
        return lax.dynamic_slice_in_dim(array, which * block, block, 1)

    def project(value, d):
        shape = jax.ShapeDtypeStruct((value.shape[0], d.shape[1]), bf16)
        return run(first_body, shape, (half,), (value, d))

    def scale_from(energy):
        return lax.rsqrt(energy / (BINS * VOXELS) + 1e-05)

    mine = lax.dynamic_slice_in_dim(patches, core * rows, rows, 0)
    dictionary2 = tie("d in", send("d", dictionary, over_cores))
    level = threshold[None, :]
    level2 = send("level", level, over_cores)
    part = project(tie("part", mine), dictionary)
    there_is["part"] = part
    other = send("f1", part, over_feat)
    raw_of = [mine, send("n1", mine, shift)]
    local_sq = jnp.sum(jnp.square(tie("square", mine).astype(f32)), axis=1)
    other_sq = send("e", local_sq, over_feat)
    part2 = project(tie("part2", mine), dictionary2)
    there_is["part2"] = part2
    other2 = send("f2", part2, over_feat)
    raw_of[1] = tie("n1 in", raw_of[1])
    raw_of.append(send("n2", raw_of[1], shift))
    level = jnp.concatenate([level, tie("level in", level2)], 1)
    scale = scale_from(local_sq + tie("e in", other_sq))
    held = tie("held in", dictionary2)
    held = run(copy_body, jax.ShapeDtypeStruct(dictionary.shape, bf16), (half,), (held,))
    there_is["held"] = held
    other, other2 = tie("f1 in", other), tie("f2 in", other2)

    half_shape = jax.ShapeDtypeStruct((step, atoms), bf16)
    away_a, away_b, misfit, start = run(
        second_body,
        (
            half_shape,
            half_shape,
            jax.ShapeDtypeStruct((rows, length), bf16),
            jax.ShapeDtypeStruct((rows, 2 * atoms), bf16),
        ),
        (half,),
        (part, other, part2, other2, mine, scale[None, :], level, dictionary, tie("second", held)),
    )
    there_is["second"] = away_a
    raw_of[2] = tie("n2 in", raw_of[2])
    raw_of.append(send("n3", raw_of[2], shift))
    back_a = send("sa", away_a, over_feat)
    back_b = send("sb", away_b, over_feat)
    base = run(
        base_body, jax.ShapeDtypeStruct((rows, atoms), f32), (half,), (tie("base", misfit), start, dictionary, held)
    )
    there_is["base"] = base

    near_level = step_rate * group_near(level, half, block)

    def codes_from(back, window):
        return soft(base[window] + step_rate * back.astype(f32), near_level).astype(bf16)

    codes_of = [codes_from(tie("sa in", back_a), slice(0, step))]
    there_is["codes a"] = codes_of[0]
    ring1 = [send("z1a", codes_of[0], shift)]
    codes_of.append(codes_from(tie("sb in", back_b), slice(step, rows)))
    there_is["codes b"] = codes_of[1]
    ring1.append(send("z1b", codes_of[1], shift))
    raw_of[3] = tie("n3 in", raw_of[3])
    ring1[0] = tie("z1a in", ring1[0])
    ring2 = [send("z2a", ring1[0], shift)]
    inside = jnp.concatenate(codes_of, 0)
    outside = send("x", inside, over_feat)
    sums = jnp.concatenate([jnp.sum(jnp.square(x.astype(f32)), axis=1) for x in raw_of[1:]])
    sums += tie("e2 in", send("e2", sums, over_feat))
    scales = scale_from(sums)
    scale_of = [scale] + [scales[k * rows : (k + 1) * rows] for k in range(n_patch - 1)]

    home_half = plane % 2
    place = jnp.where(core == plane // 2, 0, 1)
    def own_block(arrays):
        return jnp.concatenate([blocks(x, place) for x in arrays], 0)

    outside = tie("x in", outside)
    ring1[1] = tie("z1b in", ring1[1])
    ring2.append(send("z2b", ring1[1], shift))
    def whole_codes():
        both = [jnp.where(half == 0, inside, outside), jnp.where(half == 0, outside, inside)]
        upper = jnp.concatenate([x[:, :block] for x in both], 1)
        lower = send("c", jnp.concatenate([x[:, block:] for x in both], 1), over_cores)
        lower = tie("c in", lower)
        there_is["codes"] = jnp.where(
            core == 0, jnp.concatenate([upper, lower], 0), jnp.concatenate([lower, upper], 0)
        )
        return there_is["codes"]

    ring2[0] = tie("z2a in", ring2[0])
    ring3 = [send("z3a", ring2[0], shift)]
    codes = whole_codes()
    ring2[1] = tie("z2b in", ring2[1])
    ring3.append(send("z3b", ring2[1], shift))
    there1 = send("qa", own_block(ring1), over_feat)
    there2 = send("qb", own_block(ring2), over_feat)
    there1 = tie("qa in", there1)
    rings = (codes_of, ring1, ring2, ring3)

    def add_products(name, segments, kinds, totals=()):
        pieces = []
        for i, (k, c, there, _) in enumerate(segments):
            pieces += [rings[k][c], there if i else tie(name, there), raw_of[k], scale_of[k][None, :]]
        totals = run(
            functools.partial(
                sums_body, [(offset, c * step, 4 if k else 3) for k, c, _, offset in segments], tuple(kinds)
            ),
            [jax.ShapeDtypeStruct((block + length // 2, block), x) for x in kinds.values()],
            (place, half == home_half, core, place, jnp.zeros_like(place)),
            (*pieces, *totals),
            [pltpu.VMEM((len(segments) * step, size), bf16) for size in (atoms, length, block)],
        )
        there_is[name] = totals[0]
        return totals

    first = [(0, 0, outside, 0), (0, 1, outside, step), (1, 0, there1, 0), (1, 1, there1, step)]
    totals = add_products("sums1", first, {False: f32, True: f32})
    there2 = tie("qb in", there2)
    ring3[0] = tie("z3a in", ring3[0])
    there3 = [send("qc", own_block(ring3[:1]), over_feat)]
    second = [(2, 0, there2, 0), (2, 1, there2, step)]
    totals = add_products("sums2", second, {False: f32, True: f32}, totals)
    ring3[1] = tie("z3b in", ring3[1])
    there3.append(send("qd", own_block(ring3[1:]), over_feat))
    there3[0] = tie("qc in", there3[0])
    there3[1] = tie("qd in", there3[1])
    third = [(3, 0, there3[0], 0), (3, 1, there3[1], 0)]
    (total,) = add_products("sums3", third, {False: bf16}, totals[:1])
    sent = tie("sent in", send("sent", total, over_cores))
    third = [(3, 0, after(there3[0], total), 0), (3, 1, there3[1], 0)]
    (kept,) = add_products("sums4", third, {True: f32}, totals[1:])
    gram, cross = run(
        functools.partial(add_body, count),
        (jax.ShapeDtypeStruct((block, block), f32), jax.ShapeDtypeStruct((length, width), f32)),
        (half,),
        (kept, sent),
    )
    return (codes, gram, cross)


def solution(mesh):
    in_specs = (P(("slab", "patch"), "feat"), P("feat", "atom"), P("atom"))
    out_specs = (
        P(("slab", "patch"), "atom"),
        P(("slab", "atom", "feat"), "patch"),
        P(("slab", "feat"), ("patch", "atom")),
    )
    sizes = mesh.shape
    small = sizes["feat"] == 2 and sizes["atom"] == 2 and sizes["patch"] == 4
    return jax.shard_map(
        paired if small else general, mesh=mesh, in_specs=in_specs, out_specs=out_specs, check_vma=False
    )
```

```python
import functools

import jax
import jax.numpy as jnp
from jax import lax
from jax.experimental import pallas as pl
from jax.experimental.pallas import tpu as pltpu
from jax.sharding import PartitionSpec as P

BINS = 8
VOXELS = 216


step_rate = 0.2
ORDER = {
    "square": ("part",),
    "n1 out": ("part",),
    "part2": ("part",),
    "e in": ("part2",),
    "n2 out": ("part2",),
    "held in": ("part2",),
    "second": ("n1 in",),
    "sb out": ("n2 in",),
    "z1a in": ("n3 in",),
    "e2 out": ("z1a in",),
    "z2b in": ("x in", "e2 in",),
    "c out": ("z1b in",),
    "z3b in": ("sums1",),
    "z3a in": ("qa in",),
    "sb in": ("z1a out",),
    "z1b in": ("e2 in",),
    "sums2": ("codes",),
}


def soften(value, level):
    return jnp.sign(value) * jnp.maximum(jnp.abs(value) - level, 0.0)


def general(patches, dictionary, threshold):
    values = patches.astype(jnp.float32)
    local_sq = jnp.sum(values * values, axis=1)
    local_first = jnp.dot(patches, dictionary, preferred_element_type=jnp.float32)
    summed, energy = lax.psum((local_first, local_sq), "feat")
    scale = lax.rsqrt(energy[:, None] / (BINS * VOXELS) + 1e-05)
    level = step_rate * threshold[None, :]
    start = soften(step_rate * (scale * summed), level).astype(jnp.bfloat16)
    contract_last = (((1,), (1,)), ((), ()))
    own_part = lax.dot_general(start, dictionary, contract_last, preferred_element_type=jnp.float32)
    rebuilt = lax.psum(own_part, "atom")
    misfit = (scale * values - rebuilt).astype(jnp.bfloat16)
    local_second = jnp.dot(misfit, dictionary, preferred_element_type=jnp.float32)
    second = lax.psum(local_second, "feat")
    codes = soften(start.astype(jnp.float32) + step_rate * second, level).astype(jnp.bfloat16)
    codes_whole = lax.all_gather(codes, "atom", axis=1, tiled=True)
    n_patch = lax.axis_size("patch")
    n_atom = lax.axis_size("atom")
    n_feat = lax.axis_size("feat")
    total_atoms = codes_whole.shape[1]
    count = patches.shape[0] * n_patch
    contract_first = (((0,), (0,)), ((), ()))
    block_rows = total_atoms // (n_atom * n_feat)
    offset = (lax.axis_index("atom") * n_feat + lax.axis_index("feat")) * block_rows
    chosen = lax.dynamic_slice_in_dim(codes_whole, offset, block_rows, 1)
    gram_part = lax.dot_general(
        chosen, codes_whole, contract_first, preferred_element_type=jnp.float32
    )
    gram = (
        lax.psum_scatter(
            gram_part.astype(jnp.bfloat16), "patch", scatter_dimension=1, tiled=True
        ).astype(jnp.float32)
        / count
    )
    width = total_atoms // (n_patch * n_atom)
    arranged = codes_whole.reshape(codes_whole.shape[0], n_patch, n_atom, width)
    picked = lax.dynamic_slice_in_dim(arranged, lax.axis_index("atom"), 1, 2).reshape(
        codes_whole.shape[0], n_patch * width
    )
    normed = (scale * values).astype(jnp.bfloat16)
    cross_part = lax.dot_general(normed, picked, contract_first, preferred_element_type=jnp.float32)
    cross = (
        lax.psum_scatter(
            cross_part.astype(jnp.bfloat16), "patch", scatter_dimension=1, tiled=True
        ).astype(jnp.float32)
        / count
    )
    return (codes, gram, cross)


def swap(value, axis):
    return lax.ppermute(value, axis, [(0, 1), (1, 0)])


def shift(value, by=1):
    n = lax.axis_size("patch")
    return lax.ppermute(value, "patch", [(i, (i + by) % n) for i in range(n)])


def after(value, earlier):
    return lax.optimization_barrier((value, earlier))[0]


f32, bf16 = jnp.float32, jnp.bfloat16
contract_last = (((1,), (1,)), ((), ()))
contract_first = (((0,), (0,)), ((), ()))


def soft(value, level):
    return jnp.where(value > level, value - level, jnp.where(value < -level, value + level, 0.0))


def run(body, outs, scalars, arrays, scratch=()):
    fast = pl.BlockSpec(memory_space=pltpu.VMEM)
    slow = pl.BlockSpec(memory_space=pltpu.SMEM)
    return pl.pallas_call(
        body,
        out_shape=outs,
        in_specs=[slow] + [fast] * len(arrays),
        out_specs=jax.tree.map(lambda _: fast, outs),
        scratch_shapes=scratch,
        compiler_params=pltpu.CompilerParams(vmem_limit_bytes=8 << 20),
        cost_estimate=pl.CostEstimate(flops=1000, bytes_accessed=1000, transcendentals=0),
    )(jnp.stack([x.astype(jnp.int32) for x in scalars]), *arrays)


def column(row):
    n = row.shape[1]
    same = lax.broadcasted_iota(jnp.int32, (n, n), 0) == lax.broadcasted_iota(jnp.int32, (n, n), 1)
    return jnp.sum(jnp.where(same, row, 0.0), axis=1, keepdims=True)


def first_body(_, mine, d, out):
    out[...] = jnp.dot(mine[...], d[...], preferred_element_type=f32).astype(bf16)


def copy_body(_, array, out):
    out[...] = array[...]


def second_body(where, part, arrived, part2, arrived2, mine, scale, threshold, own, other, away_a, away_b, misfit, start):
    atoms = own.shape[1]
    block = atoms // 2
    step = away_a.shape[0]
    far = pl.multiple_of((1 - where[0]) * block, block)
    factor = column(scale[...])
    for i, (x, y) in enumerate(((part, arrived), (part2, arrived2))):
        columns = slice(i * atoms, (i + 1) * atoms)
        summed = x[...].astype(f32) + y[...].astype(f32)
        start[:, columns] = soft(step_rate * (factor * summed), step_rate * threshold[:, columns]).astype(bf16)
    rebuilt = sum(
        lax.dot_general(start[:, i * atoms : (i + 1) * atoms], d[...], contract_last, preferred_element_type=f32)
        for i, d in enumerate((own, other))
    )
    misfit[...] = (factor * mine[...].astype(f32) - rebuilt).astype(bf16)
    for i, d in enumerate((own, other)):
        columns = slice(i * block, (i + 1) * block)
        second = jnp.dot(misfit[...], d[:, pl.ds(far, block)], preferred_element_type=f32).astype(bf16)
        away_a[:, columns] = second[:step]
        away_b[:, columns] = second[step:]


def base_body(where, misfit, start, own, other, base):
    atoms = own.shape[1]
    block = atoms // 2
    near = pl.multiple_of(where[0] * block, block)
    for i, d in enumerate((own, other)):
        second = jnp.dot(misfit[...], d[:, pl.ds(near, block)], preferred_element_type=f32)
        known = start[:, pl.ds(pl.multiple_of(i * atoms + near, block), block)].astype(f32)
        base[:, i * block : (i + 1) * block] = known + step_rate * second


def sums_body(segments, sides_of, where, *refs):
    n = len(segments)
    m = len(sides_of)
    pieces, totals = refs[: 4 * n], refs[4 * n : -3 - m]
    outs, (lhs, sides, right) = refs[-3 - m : -3], refs[-3:]
    block = right.shape[1]
    width = block // 2
    place = pl.multiple_of(where[0] * block, block)
    here = where[1] == 1
    step = lhs.shape[0] // n
    for k, (offset, base, entry) in enumerate(segments):
        x, there, raw, scale = pieces[4 * k : 4 * k + 4]
        window = slice(k * step, (k + 1) * step)
        lhs[window, :] = x[...]
        spot = pl.multiple_of(where[entry] * block, block)
        right[window, :] = jnp.where(
            here, x[:, pl.ds(place, block)], there[offset : offset + step, pl.ds(spot, block)]
        )
        factor = column(scale[...])[base : base + step]
        sides[window, :] = (factor * raw[base : base + step, :].astype(f32)).astype(bf16)
    mine = pl.multiple_of(where[2] * width, width)
    theirs = pl.multiple_of((1 - where[2]) * width, width)
    tall = sides.shape[1] // 2

    def product(a, b):
        return lax.dot_general(a, b, contract_first, preferred_element_type=f32)

    for i, ours in enumerate(sides_of):
        left, columns = (slice(0, block), mine) if ours else (slice(block, 2 * block), theirs)
        for window, value in (
            ((slice(0, block), slice(0, block)), product(lhs[:, left], right[...])),
            ((slice(block, block + tall), slice(0, width)), product(sides[:, :tall], right[:, pl.ds(columns, width)])),
            ((slice(block, block + tall), slice(width, block)), product(sides[:, tall:], right[:, pl.ds(columns, width)])),
        ):
            if totals:
                value += totals[i][window]
            outs[i][window] = value.astype(outs[i].dtype)


def add_body(count, _, kept, sent, gram, cross):
    block = gram.shape[0]
    width = cross.shape[1]
    tall = cross.shape[0] // 2
    gram[...] = (kept[:block, :] + sent[:block, :].astype(f32)) * (1.0 / count)
    for i in range(2):
        window = slice(i * width, (i + 1) * width)
        total = kept[block:, window] + sent[block:, window].astype(f32)
        cross[i * tall : (i + 1) * tall, :] = total * (1.0 / count)


def group_near(level, half, block):
    atoms = 2 * block
    parts = [lax.dynamic_slice_in_dim(level, i * atoms + half * block, block, 1) for i in range(2)]
    return jnp.concatenate(parts, 1)


def paired(patches, dictionary, threshold):
    n_patch = lax.axis_size("patch")
    plane = lax.axis_index("patch")
    core = lax.axis_index("atom")
    half = lax.axis_index("feat")
    count = patches.shape[0] * n_patch
    length = patches.shape[1]
    rows = patches.shape[0] // 2
    atoms = dictionary.shape[1]
    block = atoms // 2
    width = block // 2
    step = rows // 2
    there_is = {}

    def tie(name, value):
        earlier = [there_is[x] for x in ORDER.get(name, ())]
        there_is[name] = after(value, earlier) if earlier else value
        return there_is[name]

    def send(name, value, how):
        return how(tie(name + " out", value))

    def over_feat(value):
        return swap(value, "feat")

    def over_cores(value):
        return swap(value, "atom")

    def blocks(array, which):
        return lax.dynamic_slice_in_dim(array, which * block, block, 1)

    def project(value, d):
        shape = jax.ShapeDtypeStruct((value.shape[0], d.shape[1]), bf16)
        return run(first_body, shape, (half,), (value, d))

    def scale_from(energy):
        return lax.rsqrt(energy / (BINS * VOXELS) + 1e-05)

    mine = lax.dynamic_slice_in_dim(patches, core * rows, rows, 0)
    dictionary2 = tie("d in", send("d", dictionary, over_cores))
    level = threshold[None, :]
    level2 = send("level", level, over_cores)
    part = project(tie("part", mine), dictionary)
    there_is["part"] = part
    other = send("f1", part, over_feat)
    raw_of = [mine, send("n1", mine, shift)]
    local_sq = jnp.sum(jnp.square(tie("square", mine).astype(f32)), axis=1)
    other_sq = send("e", local_sq, over_feat)
    part2 = project(tie("part2", mine), dictionary2)
    there_is["part2"] = part2
    other2 = send("f2", part2, over_feat)
    raw_of[1] = tie("n1 in", raw_of[1])
    raw_of.append(send("n2", raw_of[1], shift))
    level = jnp.concatenate([level, tie("level in", level2)], 1)
    scale = scale_from(local_sq + tie("e in", other_sq))
    held = tie("held in", dictionary2)
    held = run(copy_body, jax.ShapeDtypeStruct(dictionary.shape, bf16), (half,), (held,))
    there_is["held"] = held
    other, other2 = tie("f1 in", other), tie("f2 in", other2)

    half_shape = jax.ShapeDtypeStruct((step, atoms), bf16)
    away_a, away_b, misfit, start = run(
        second_body,
        (
            half_shape,
            half_shape,
            jax.ShapeDtypeStruct((rows, length), bf16),
            jax.ShapeDtypeStruct((rows, 2 * atoms), bf16),
        ),
        (half,),
        (part, other, part2, other2, mine, scale[None, :], level, dictionary, tie("second", held)),
    )
    there_is["second"] = away_a
    raw_of[2] = tie("n2 in", raw_of[2])
    raw_of.append(send("n3", raw_of[2], shift))
    back_a = send("sa", away_a, over_feat)
    back_b = send("sb", away_b, over_feat)
    base = run(
        base_body, jax.ShapeDtypeStruct((rows, atoms), f32), (half,), (tie("base", misfit), start, dictionary, held)
    )
    there_is["base"] = base

    near_level = step_rate * group_near(level, half, block)

    def codes_from(back, window):
        return soft(base[window] + step_rate * back.astype(f32), near_level).astype(bf16)

    codes_of = [codes_from(tie("sa in", back_a), slice(0, step))]
    there_is["codes a"] = codes_of[0]
    ring1 = [send("z1a", codes_of[0], shift)]
    codes_of.append(codes_from(tie("sb in", back_b), slice(step, rows)))
    there_is["codes b"] = codes_of[1]
    ring1.append(send("z1b", codes_of[1], shift))
    raw_of[3] = tie("n3 in", raw_of[3])
    ring1[0] = tie("z1a in", ring1[0])
    ring2 = [send("z2a", ring1[0], shift)]
    inside = jnp.concatenate(codes_of, 0)
    outside = send("x", inside, over_feat)
    sums = jnp.concatenate([jnp.sum(jnp.square(x.astype(f32)), axis=1) for x in raw_of[1:]])
    sums += tie("e2 in", send("e2", sums, over_feat))
    scales = scale_from(sums)
    scale_of = [scale] + [scales[k * rows : (k + 1) * rows] for k in range(n_patch - 1)]

    home_half = plane % 2
    place = jnp.where(core == plane // 2, 0, 1)
    def own_block(arrays):
        return jnp.concatenate([blocks(x, place) for x in arrays], 0)

    outside = tie("x in", outside)
    ring1[1] = tie("z1b in", ring1[1])
    ring2.append(send("z2b", ring1[1], shift))
    def whole_codes():
        both = [jnp.where(half == 0, inside, outside), jnp.where(half == 0, outside, inside)]
        upper = jnp.concatenate([x[:, :block] for x in both], 1)
        lower = send("c", jnp.concatenate([x[:, block:] for x in both], 1), over_cores)
        lower = tie("c in", lower)
        there_is["codes"] = jnp.where(
            core == 0, jnp.concatenate([upper, lower], 0), jnp.concatenate([lower, upper], 0)
        )
        return there_is["codes"]

    ring2[0] = tie("z2a in", ring2[0])
    ring3 = [send("z3a", ring2[0], shift)]
    codes = whole_codes()
    ring2[1] = tie("z2b in", ring2[1])
    ring3.append(send("z3b", ring2[1], shift))
    there1 = send("qa", own_block(ring1), over_feat)
    there2 = send("qb", own_block(ring2), over_feat)
    there1 = tie("qa in", there1)
    rings = (codes_of, ring1, ring2, ring3)

    def add_products(name, segments, kinds, totals=()):
        pieces = []
        for i, (k, c, there, _) in enumerate(segments):
            pieces += [rings[k][c], there if i else tie(name, there), raw_of[k], scale_of[k][None, :]]
        totals = run(
            functools.partial(
                sums_body, [(offset, c * step, 4 if k else 3) for k, c, _, offset in segments], tuple(kinds)
            ),
            [jax.ShapeDtypeStruct((block + length // 2, block), x) for x in kinds.values()],
            (place, half == home_half, core, place, jnp.zeros_like(place)),
            (*pieces, *totals),
            [pltpu.VMEM((len(segments) * step, size), bf16) for size in (atoms, length, block)],
        )
        there_is[name] = totals[0]
        return totals

    first = [(0, 0, outside, 0), (0, 1, outside, step), (1, 0, there1, 0), (1, 1, there1, step)]
    totals = add_products("sums1", first, {False: f32, True: f32})
    there2 = tie("qb in", there2)
    ring3[0] = tie("z3a in", ring3[0])
    there3 = [send("qc", own_block(ring3[:1]), over_feat)]
    second = [(2, 0, there2, 0), (2, 1, there2, step), (3, 0, there3[0], 0)]
    totals = add_products("sums2", second, {False: f32, True: f32}, totals)
    ring3[1] = tie("z3b in", ring3[1])
    there3.append(send("qd", own_block(ring3[1:]), over_feat))
    there3[0] = tie("qc in", there3[0])
    there3[1] = tie("qd in", there3[1])
    third = [(3, 1, there3[1], 0)]
    (total,) = add_products("sums3", third, {False: bf16}, totals[:1])
    sent = tie("sent in", send("sent", total, over_cores))
    third = [(3, 1, after(there3[1], total), 0)]
    (kept,) = add_products("sums4", third, {True: f32}, totals[1:])
    gram, cross = run(
        functools.partial(add_body, count),
        (jax.ShapeDtypeStruct((block, block), f32), jax.ShapeDtypeStruct((length, width), f32)),
        (half,),
        (kept, sent),
    )
    return (codes, gram, cross)


def solution(mesh):
    in_specs = (P(("slab", "patch"), "feat"), P("feat", "atom"), P("atom"))
    out_specs = (
        P(("slab", "patch"), "atom"),
        P(("slab", "atom", "feat"), "patch"),
        P(("slab", "feat"), ("patch", "atom")),
    )
    sizes = mesh.shape
    small = sizes["feat"] == 2 and sizes["atom"] == 2 and sizes["patch"] == 4
    return jax.shard_map(
        paired if small else general, mesh=mesh, in_specs=in_specs, out_specs=out_specs, check_vma=False
    )
```
